32 devices in a mesh: section: 4 (over y, x), expert: 8 (over z, core).
Axes of the slice: x: 2, y: 2, z: 4, core: 2. Of those that a mesh axis runs over, the one named last changes fastest.
Arguments:
- hidden_in: bfloat16 [4, 1024, 2880], P('section', 'expert')
- norm_gain: float32 [4, 2880], P('section'), may hold values from 0.25 to 1.75
- out_grad: bfloat16 [4, 1024, 2880], P('section', 'expert'), may hold values from -6 to 6
- expert_ids: int32 [4, 1024, 4], P('section', 'expert'), may hold values from 0 to 7, all different within a row; in each aligned block of 128 rows (0 to 127, 128 to 255, ..., all dimensions but the last counted through in order) at most 80 rows name the same one
- route_weights: float32 [4, 1024, 4], P('section', 'expert'), may hold values from 0 to 1, as said below
- w_gate_up: bfloat16 [4, 8, 2880, 2880], P('section', 'expert'), may hold values from -0.109375 to 0.109375
- w_down: bfloat16 [4, 8, 1440, 2880], P('section', 'expert'), may hold values from -0.15625 to 0.15625
Outputs:
- input_grad: bfloat16 [4, 1024, 2880], P('section', 'expert')
The draws below stay inside these ranges and needn't reach their ends.
Inputs may be any that keep to these rules, and one draw needn't show every extreme that they name: `expert_ids`: each token names 4 different experts. The 128 tokens of one index of expert in one section name any one expert at most 80 times, a bound that some block reaches. `route_weights`: each token's 4 weights are positive and sum to one.
All inputs are finite; a program needn't handle non-finite values.
Results may differ from the reference program's by a relative error of at most 0.0047.
Values may be sent and summed in bfloat16 or wider, within the bound.
A program may use at most 128 MiB of HBM per device.

```python
import math
import jax
import jax.numpy as jnp
import numpy as np
from jax import lax

D = 2880
FFW = 1440
TOPK = 4
TOK_DEV = 128
SECTIONS = 4
EXPERTS = 8
TOKENS = 1024
CAP = 80


def draw_hidden_in(key, part):
    keys = jax.random.split(key, 3)
    row_scale = jnp.exp(jax.random.uniform(keys[1], (SECTIONS, TOKENS, 1), jnp.float32, jnp.log(0.5), jnp.log(5.0)))
    col_scale = jnp.exp(jax.random.uniform(keys[2], (1, 1, D), jnp.float32, jnp.log(0.3), jnp.log(3.0)))
    base = jax.random.normal(keys[0], (SECTIONS, TOKENS, D), jnp.float32)
    return (base * row_scale * col_scale).astype(jnp.bfloat16)


def draw_route_weights(key, part):
    logits = jax.random.normal(key, (SECTIONS, TOKENS, TOPK), jnp.float32)
    return jax.nn.softmax(logits, axis=-1)


def level_of(key, dims, cuts, least, largest):
    factor_of, own = 1.0, jax.random.fold_in(key, 6)
    for dim, blocks in cuts:
        heights = jnp.exp(jax.random.uniform(jax.random.fold_in(own, dim), (blocks,), jnp.float32, least / len(cuts), largest / len(cuts)))
        factor_of = factor_of * jnp.repeat(heights, dims[dim] // blocks).reshape([-1 if axis == dim else 1 for axis in range(len(dims))])
    return factor_of


def routed_block(key, own, number, rows, amount, top, reach, lean):
    sequence = jax.random.permutation(key, amount)
    crowded, ordinary = portions_of(amount, rows * top, reach, lean, True), portions_of(amount, rows * top, reach, lean, False)
    places = jnp.arange(amount)

    def named(sizes, turn):
        used = int((sizes > 0).sum())
        fixed = max(1, used // 4)
        shifted = fixed + (places - fixed + turn * (used - fixed)) % max(1, amount - fixed)
        return jnp.zeros((amount,), jnp.int32).at[sequence[jnp.where(places < fixed, places, shifted)]].set(jnp.asarray(sizes, jnp.int32))

    sizes = jnp.where(number % 4 == 0, named(crowded, number // 4), named(ordinary, number - number // 4 - 1))
    mixed = jax.random.permutation(jax.random.fold_in(own, 3), amount)
    giver, taker = mixed[0:amount // 2 * 2:2], mixed[1:amount // 2 * 2:2]
    margin = jnp.minimum(sizes[giver] - 1, reach - sizes[taker]) // 2
    margin = jnp.where((giver == sequence[0]) | (taker == sequence[0]) | (sizes[taker] == 0), 0, jnp.maximum(margin, 0))
    shifted = jax.random.randint(jax.random.fold_in(own, 4), (amount // 2,), 0, 1 << 20) % (margin + 1)
    sizes = sizes.at[giver].add(-shifted).at[taker].add(shifted)
    items = jnp.searchsorted(jnp.cumsum(sizes), jnp.arange(rows * top), side="right").astype(jnp.int32)
    table = items.reshape(top, rows).T
    table = table[jax.random.permutation(jax.random.fold_in(own, 1), rows)]
    turn = jax.random.randint(jax.random.fold_in(own, 2), (rows, 1), 0, top)
    return jnp.take_along_axis(table, (jnp.arange(top)[None, :] + turn) % top, axis=1)


def portions_of(number_of, total, most, lean, full):
    weights = [(1 << 20) // math.isqrt(rank ** lean) + 1 for rank in range(1, number_of + 1)]
    largest = most if full else min(most, max(-(-total // number_of), total * weights[0] // sum(weights)))
    least = 1 if total - largest >= number_of - 1 else 0
    holding, rest = [largest] + [least] * (number_of - 1), total - largest - least * (number_of - 1)
    while rest > 0:
        free = [i for i in range(1, number_of) if holding[i] < largest] or [i for i in range(1, number_of) if holding[i] < most]
        mass, left = sum([weights[i] for i in free]), rest
        for i in free:
            addition = min(most - holding[i], max(1, left * weights[i] // mass), rest)
            holding[i] = holding[i] + addition
            rest = rest - addition
    return np.array(holding)


def scatter_about(rng, shape, spread, most, pieces=(), kind=jnp.bfloat16):
    drawn = jax.random.normal(rng, shape, jnp.float32) * spread
    if len(pieces) > 0:
        drawn = level_of(rng, shape, pieces, -0.22, 0.18) * drawn
    return jnp.clip(drawn, min=-most, max=most).astype(kind)


def setup_inputs(seed: int = 0) -> dict:
    arg_keys = jax.random.split(jax.random.key(seed), 8)
    hidden_in = draw_hidden_in(jax.random.fold_in(arg_keys[7], 71), 0)
    norm_gain = jnp.clip(1.0 + 0.15 * jax.random.normal(arg_keys[1], (SECTIONS, D), jnp.float32), 0.25, 1.75)
    out_grad = scatter_about(arg_keys[2], (SECTIONS, TOKENS, D), 1.0, 6.0, ((0, 4), (1, 8)))
    expert_ids_keys = jax.random.split(jax.random.fold_in(arg_keys[3], 1), SECTIONS * TOKENS // TOK_DEV)
    expert_ids_turns = jax.random.permutation(jax.random.fold_in(arg_keys[3], 3), SECTIONS * TOKENS // TOK_DEV)
    expert_ids = jax.vmap(lambda own, number: routed_block(jax.random.fold_in(arg_keys[3], 2), own, number, TOK_DEV, EXPERTS, TOPK, CAP, 2))(expert_ids_keys, expert_ids_turns).reshape((SECTIONS, TOKENS, TOPK))
    route_weights = draw_route_weights(jax.random.fold_in(arg_keys[7], 71), 0)
    w_gate_up = scatter_about(arg_keys[5], (SECTIONS, EXPERTS, D, 2 * FFW), D ** -0.5, 0.109375, ((0, 4), (1, 8)))
    w_down = scatter_about(arg_keys[6], (SECTIONS, EXPERTS, FFW, D), FFW ** -0.5, 0.15625, ((0, 4), (1, 8)))
    return dict(hidden_in=hidden_in, norm_gain=norm_gain, out_grad=out_grad, expert_ids=expert_ids, route_weights=route_weights, w_gate_up=w_gate_up, w_down=w_down)


glu_alpha = 1.702
norm_eps = 1e-05

def expert_backward(packed):
    rows_in, grad_rows, gate_up, down_proj = packed
    preact = jnp.dot(rows_in, gate_up, preferred_element_type=jnp.float32)
    dact = jnp.dot(grad_rows, down_proj.T, preferred_element_type=jnp.float32)
    half = down_proj.shape[0]
    gate = preact[:, :half]
    up_part = preact[:, half:]
    sig = jax.nn.sigmoid(glu_alpha * gate)
    dgate = dact * (up_part + 1.0) * (sig + glu_alpha * gate * sig * (1.0 - sig))
    dup = dact * gate * sig
    dpre = jnp.concatenate([dgate, dup], axis=1).astype(jnp.bfloat16)
    return jnp.dot(dpre, gate_up.T, preferred_element_type=jnp.float32).astype(jnp.bfloat16)

def section_pass(tokens, gain_vector_row, incoming_gradient, routes, weights, gate_up, down_proj):
    input_single_precision = tokens.astype(jnp.float32)
    inverse_root_mean = lax.rsqrt(lax.optimization_barrier(jnp.mean(input_single_precision * input_single_precision, axis=-1, keepdims=True)) + norm_eps)
    normalized_input = input_single_precision * inverse_root_mean
    rescaled_input = (normalized_input * gain_vector_row[None, :]).astype(jnp.bfloat16)
    tok_count = tokens.shape[0]
    flat_ids = routes.reshape(-1).astype(jnp.int32)
    assign = flat_ids.shape[0]
    one_hot = (flat_ids[:, None] == jnp.arange(EXPERTS, dtype=jnp.int32)[None, :]).astype(jnp.int32)
    slot_rank = lax.optimization_barrier(jnp.sum((jnp.cumsum(one_hot, axis=0) - one_hot) * one_hot, axis=1)).astype(jnp.int32)
    per_expert = EXPERTS * CAP
    slot_index = (flat_ids * per_expert + slot_rank).astype(jnp.int32)
    source_of = jnp.full((EXPERTS * per_expert,), assign, jnp.int32).at[slot_index].set(jnp.arange(assign, dtype=jnp.int32))
    token_of = (source_of // TOPK).astype(jnp.int32)
    normed_pad = jnp.concatenate([rescaled_input, jnp.zeros((1, D), jnp.bfloat16)], axis=0)
    grad_pad = jnp.concatenate([incoming_gradient.astype(jnp.float32), jnp.zeros((1, D), jnp.float32)], axis=0)
    weight_pad = jnp.concatenate([weights.reshape(-1).astype(jnp.float32), jnp.zeros((1,), jnp.float32)])
    rows_in = normed_pad[token_of].reshape(EXPERTS, per_expert, D)
    grad_rows = (weight_pad[source_of][:, None] * grad_pad[token_of]).astype(jnp.bfloat16).reshape(EXPERTS, per_expert, D)
    slots = lax.map(expert_backward, (rows_in, grad_rows, gate_up, down_proj))
    gathered = slots.reshape(-1, D)[slot_index].astype(jnp.float32)
    dnorm = lax.optimization_barrier(jnp.sum(gathered.reshape(tok_count, TOPK, D), axis=1))
    normalized_input_gradient = dnorm * gain_vector_row[None, :]
    projected_rows = lax.optimization_barrier(jnp.mean(normalized_input_gradient * normalized_input, axis=-1, keepdims=True))
    return (incoming_gradient.astype(jnp.float32) + inverse_root_mean * (normalized_input_gradient - normalized_input * projected_rows)).astype(jnp.bfloat16)

def reference(hidden_in, norm_gain, out_grad, expert_ids, route_weights, w_gate_up, w_down):
    results = []
    for section_num in range(SECTIONS):
        results.append(section_pass(hidden_in[section_num], norm_gain[section_num], out_grad[section_num], expert_ids[section_num], route_weights[section_num], w_gate_up[section_num], w_down[section_num]))
    stacked = jnp.stack(results, axis=0)
    return jnp.roll(stacked, -1, axis=0)
```

```python
import functools
import jax
import jax.numpy as jnp
from jax import lax
from jax.experimental import pallas as pl
from jax.experimental.pallas import tpu as pltpu
from jax.sharding import PartitionSpec as P

glu_alpha = 1.702
norm_eps = 1e-05
vmem_bytes = 60 * 1024 * 1024


def spans(total, width):
    return [(start, min(start + width, total)) for start in range(0, total, width)]


def shifted(value, axis, steps):
    count = lax.axis_size(axis)
    pairs = [(source, (source + steps) % count) for source in range(count)]
    return lax.ppermute(value, axis, pairs)


def block_kernel(
    chips,
    x_hbm, g_hbm, wtab_hbm, gate_up_hbm, down_hbm, out_ref,
    xs, gs, wtab, ws, gate_up, down, pre, act, res, cross_in, line_in,
    load_sems, recv_x, recv_g, recv_w, send_w,
    up_x, up_g, dn_x, dn_g, cr_x, cr_g,
    cross_recv, cross_send, line_recv, line_send,
):
    me = lax.axis_index("expert")
    p = me // 2
    c = me % 2
    other = 1 - c
    count = 2 * chips
    rows, width = x_hbm.shape
    half = down_hbm.shape[0]
    out_spans = spans(width, 768)

    def device(chip, core):
        return {"expert": 2 * chip + core}

    load_x = pltpu.make_async_copy(x_hbm, xs.at[me], load_sems.at[0])
    load_g = pltpu.make_async_copy(g_hbm, gs.at[me], load_sems.at[1])
    load_w = pltpu.make_async_copy(wtab_hbm, wtab, load_sems.at[2])
    load_gate_up = pltpu.make_async_copy(gate_up_hbm, gate_up, load_sems.at[3])
    load_down = pltpu.make_async_copy(down_hbm, down, load_sems.at[4])
    load_x.start()
    load_g.start()
    load_w.start()
    load_gate_up.start()
    load_down.start()

    barrier = pltpu.get_barrier_semaphore()

    @pl.loop(1, count)
    def _(step):
        pl.semaphore_signal(barrier, inc=1, device_id={"expert": (me + step) % count})

    pl.semaphore_wait(barrier, count - 1)

    def gather_copy(buf, slot, send, recv, chip, core):
        return pltpu.make_async_remote_copy(
            src_ref=buf.at[slot], dst_ref=buf.at[slot],
            send_sem=send.at[slot], recv_sem=recv.at[slot],
            device_id=device(chip, core),
        )

    def weight_copy(target):
        return pltpu.make_async_remote_copy(
            src_ref=wtab.at[target], dst_ref=ws.at[me],
            send_sem=send_w.at[target], recv_sem=recv_w.at[me],
            device_id={"expert": target},
        )

    def weight_arrival(source):
        return pltpu.make_async_remote_copy(
            src_ref=wtab.at[source], dst_ref=ws.at[source],
            send_sem=send_w.at[source], recv_sem=recv_w.at[source],
            device_id={"expert": source},
        )

    def up_copy(buf, slot, send, recv):
        return gather_copy(buf, slot, send, recv, jnp.minimum(p + 1, chips - 1), c)

    def down_copy(buf, slot, send, recv):
        return gather_copy(buf, slot, send, recv, jnp.maximum(p - 1, 0), c)

    def core_copy(buf, slot, send, recv):
        return gather_copy(buf, slot, send, recv, p, other)

    def send_own(buf, up_sem, dn_sem, recv):
        @pl.when(p < chips - 1)
        def _():
            up_copy(buf, me, up_sem, recv).start()

        @pl.when(p > 0)
        def _():
            down_copy(buf, me, dn_sem, recv).start()

    def pass_on(k, buf, up_sem, dn_sem, cr_sem, recv):
        @pl.when(p - k >= 0)
        def _():
            slot = 2 * (p - k) + c
            core_copy(buf, slot, cr_sem, recv).wait_recv()
            core_copy(buf, slot, cr_sem, recv).start()

            @pl.when(p < chips - 1)
            def _():
                up_copy(buf, slot, up_sem, recv).start()

        @pl.when(p + k < chips)
        def _():
            slot = 2 * (p + k) + c
            core_copy(buf, slot, cr_sem, recv).wait_recv()
            core_copy(buf, slot, cr_sem, recv).start()

            @pl.when(p > 0)
            def _():
                down_copy(buf, slot, dn_sem, recv).start()

    def cross_copy(q, t):
        first, last = out_spans[t]
        return pltpu.make_async_remote_copy(
            src_ref=res.at[2 * q + other, :, pl.ds(first, last - first)],
            dst_ref=cross_in.at[q, :, pl.ds(first, last - first)],
            send_sem=cross_send.at[q, t], recv_sem=cross_recv.at[q, t],
            device_id=device(p, other),
        )

    def cross_arrival(q, t):
        return cross_copy(q, t)

    def line_copy(q, t):
        first, last = out_spans[t]
        toward = jnp.where(q > p, jnp.minimum(p + 1, chips - 1), jnp.maximum(p - 1, 0))
        slot = jnp.where(q > p, 0, 1)
        return pltpu.make_async_remote_copy(
            src_ref=res.at[2 * q + c, :, pl.ds(first, last - first)],
            dst_ref=line_in.at[slot, q, :, pl.ds(first, last - first)],
            send_sem=line_send.at[q, t], recv_sem=line_recv.at[slot, q, t],
            device_id=device(toward, c),
        )

    def line_arrival(slot, q, t):
        first, last = out_spans[t]
        return pltpu.make_async_remote_copy(
            src_ref=res.at[2 * q + c, :, pl.ds(first, last - first)],
            dst_ref=line_in.at[slot, q, :, pl.ds(first, last - first)],
            send_sem=line_send.at[q, t], recv_sem=line_recv.at[slot, q, t],
            device_id=device(p, other),
        )

    def combine(q, t):
        first, last = out_spans[t]
        cross_arrival(q, t).wait_recv()
        summed = res[2 * q + c, :, first:last].astype(jnp.float32) + cross_in[
            q, :, first:last
        ].astype(jnp.float32)
        res[2 * q + c, :, first:last] = summed.astype(jnp.bfloat16)
        starts = ((p == chips - 1) & (q < p)) | ((p == 0) & (q > p))

        @pl.when(starts)
        def _():
            line_copy(q, t).start()

    load_x.wait()
    core_copy(xs, me, cr_x, recv_x).start()
    send_own(xs, up_x, dn_x, recv_x)
    load_g.wait()
    core_copy(gs, me, cr_g, recv_g).start()
    load_w.wait()

    @pl.loop(1, count)
    def _(step):
        weight_copy((me + step) % count).start()

    ws[pl.ds(me, 1)] = wtab[pl.ds(me, 1)]
    load_gate_up.wait()
    load_down.wait()

    @pl.loop(1, count)
    def _(step):
        weight_arrival((me + step) % count).wait_recv()

    def forward_part(q):
        core_copy(xs, 2 * q + other, cr_x, recv_x).wait_recv()
        inputs = xs[pl.ds(2 * q, 2)].reshape(2 * rows, width)
        for first, last in spans(2 * half, 512):
            pre[:, first:last] = jnp.dot(
                inputs, gate_up[:, first:last], preferred_element_type=jnp.float32
            )

    def backward_part(q):
        core_copy(gs, 2 * q + other, cr_g, recv_g).wait_recv()
        diagonal = lax.broadcasted_iota(jnp.int32, (rows, rows), 0) == lax.broadcasted_iota(
            jnp.int32, (rows, rows), 1
        )
        for core in range(2):
            across = jnp.broadcast_to(ws[2 * q + core], (rows, rows))
            column = jnp.sum(jnp.where(diagonal, across, 0.0), axis=1, keepdims=True)
            act[core * rows:(core + 1) * rows, :] = (
                column * gs[2 * q + core].astype(jnp.float32)
            ).astype(jnp.bfloat16)
        for first, last in spans(half, 512):
            dact = lax.dot_general(
                act[...], down[first:last, :], (((1,), (1,)), ((), ())),
                preferred_element_type=jnp.float32,
            )
            gate = pre[:, first:last]
            up_part = pre[:, half + first:half + last]
            sig = jax.nn.sigmoid(glu_alpha * gate)
            pre[:, first:last] = dact * (up_part + 1.0) * (
                sig + glu_alpha * gate * sig * (1.0 - sig)
            )
            pre[:, half + first:half + last] = dact * gate * sig
        act[...] = pre[...].astype(jnp.bfloat16)
        for t, (first, last) in enumerate(out_spans):
            part = lax.dot_general(
                act[...], gate_up[first:last, :], (((1,), (1,)), ((), ())),
                preferred_element_type=jnp.float32,
            ).astype(jnp.bfloat16)
            res[pl.ds(2 * q, 2), :, first:last] = part.reshape(2, rows, last - first)
            cross_copy(q, t).start()
            if t > 0:
                combine(q, t - 1)
        combine(q, len(out_spans) - 1)

    @pl.loop(0, 2 * chips - 1)
    def _(i):
        k = (i + 1) // 2
        leading = i % 2 == 1
        q = jnp.where(leading, p - k, p + k)
        valid = (q >= 0) & (q < chips)

        @pl.when(leading)
        def _():
            pass_on(k, xs, up_x, dn_x, cr_x, recv_x)

        @pl.when(valid)
        def _():
            forward_part(q)

        @pl.when(leading)
        def _():
            pass_on(k, gs, up_g, dn_g, cr_g, recv_g)

        @pl.when(i == 0)
        def _():
            send_own(gs, up_g, dn_g, recv_g)

        @pl.when(valid)
        def _():
            backward_part(q)

    def relay(slot, q, t):
        first, last = out_spans[t]
        line_arrival(slot, q, t).wait_recv()
        summed = res[2 * q + c, :, first:last].astype(jnp.float32) + line_in[
            slot, q, :, first:last
        ].astype(jnp.float32)
        res[2 * q + c, :, first:last] = summed.astype(jnp.bfloat16)
        line_copy(q, t).start()

    inner = (p > 0) & (p < chips - 1)
    near_low = p < chips // 2
    for distance in range(1, chips):
        for t in range(len(out_spans)):
            for turn in range(2):
                slot = jnp.where(near_low, turn, 1 - turn)
                q = jnp.where(slot == 0, distance, chips - 1 - distance)
                ahead = jnp.where(slot == 0, q > p, q < p)

                @pl.when(inner & ahead)
                def _(slot=slot, q=q, t=t):
                    relay(slot, q, t)

    for t, (first, last) in enumerate(out_spans):
        out_ref[:, first:last] = res[me, :, first:last].astype(jnp.float32)

        @pl.when(p > 0)
        def _(t=t, first=first, last=last):
            line_arrival(0, p, t).wait_recv()
            out_ref[:, first:last] += line_in[0, p, :, first:last].astype(jnp.float32)

        @pl.when(p < chips - 1)
        def _(t=t, first=first, last=last):
            line_arrival(1, p, t).wait_recv()
            out_ref[:, first:last] += line_in[1, p, :, first:last].astype(jnp.float32)

    @pl.loop(1, count)
    def _(step):
        weight_copy((me + step) % count).wait_send()

    @pl.loop(0, chips)
    def _(q):
        slot = 2 * q + c
        core_copy(xs, slot, cr_x, recv_x).wait_send()
        core_copy(gs, slot, cr_g, recv_g).wait_send()

        @pl.when((q <= p) & (p < chips - 1))
        def _():
            up_copy(xs, slot, up_x, recv_x).wait_send()
            up_copy(gs, slot, up_g, recv_g).wait_send()

        @pl.when((q >= p) & (p > 0))
        def _():
            down_copy(xs, slot, dn_x, recv_x).wait_send()
            down_copy(gs, slot, dn_g, recv_g).wait_send()

        for t in range(len(out_spans)):
            cross_copy(q, t).wait_send()

            @pl.when(q != p)
            def _(t=t):
                line_copy(q, t).wait_send()


def line_backward(normed, grads, weight_table, gate_up, down_proj):
    count = weight_table.shape[0]
    chips = count // 2
    rows, width = normed.shape
    half = down_proj.shape[0]
    pieces = len(spans(width, 768))
    dma = pltpu.SemaphoreType.DMA
    flops = 2 * count * rows * width * 5 * half
    return pl.pallas_call(
        functools.partial(block_kernel, chips),
        out_shape=jax.ShapeDtypeStruct((rows, width), jnp.float32),
        in_specs=[pl.BlockSpec(memory_space=pl.ANY)] * 5,
        out_specs=pl.BlockSpec(memory_space=pltpu.VMEM),
        scratch_shapes=[
            pltpu.VMEM((count, rows, width), jnp.bfloat16),
            pltpu.VMEM((count, rows, width), jnp.bfloat16),
            pltpu.VMEM((count, 1, rows), jnp.float32),
            pltpu.VMEM((count, 1, rows), jnp.float32),
            pltpu.VMEM((width, 2 * half), jnp.bfloat16),
            pltpu.VMEM((half, width), jnp.bfloat16),
            pltpu.VMEM((2 * rows, 2 * half), jnp.float32),
            pltpu.VMEM((2 * rows, width), jnp.bfloat16),
            pltpu.VMEM((count, rows, width), jnp.bfloat16),
            pltpu.VMEM((chips, rows, width), jnp.bfloat16),
            pltpu.VMEM((2, chips, rows, width), jnp.bfloat16),
            dma((5,)),
            dma((count,)), dma((count,)), dma((count,)), dma((count,)),
            dma((count,)), dma((count,)), dma((count,)), dma((count,)),
            dma((count,)), dma((count,)),
            dma((chips, pieces)), dma((chips, pieces)),
            dma((2, chips, pieces)), dma((chips, pieces)),
        ],
        compiler_params=pltpu.CompilerParams(
            collective_id=0, has_side_effects=True, vmem_limit_bytes=vmem_bytes
        ),
        cost_estimate=pl.CostEstimate(
            flops=flops, bytes_accessed=10 * half * width, transcendentals=0
        ),
    )(normed, grads, weight_table, gate_up, down_proj)


def expert_backward(rows_in, grad_rows, gate_up, down_proj):
    preact = jnp.dot(rows_in, gate_up, preferred_element_type=jnp.float32)
    dact = lax.dot_general(
        grad_rows, down_proj, (((1,), (1,)), ((), ())), preferred_element_type=jnp.float32
    )
    half = down_proj.shape[0]
    gate = preact[:, :half]
    up_part = preact[:, half:]
    sig = jax.nn.sigmoid(glu_alpha * gate)
    dgate = dact * (up_part + 1.0) * (sig + glu_alpha * gate * sig * (1.0 - sig))
    dup = dact * gate * sig
    dpre = jnp.concatenate([dgate, dup], axis=1).astype(jnp.bfloat16)
    result = lax.dot_general(
        dpre, gate_up, (((1,), (1,)), ((), ())), preferred_element_type=jnp.float32
    )
    return result.astype(jnp.bfloat16)


def slab_exchange(slab):
    return lax.all_to_all(slab, "expert", split_axis=0, concat_axis=0, tiled=True)


def slab_backward(normed, grads, routes, weights, gate_up, down_proj, experts):
    tok_count, feat_width = normed.shape
    top_count = routes.shape[1]
    capacity = max(2, tok_count * top_count * 5 // (4 * experts))
    flat_ids = routes.reshape(-1)
    assign = flat_ids.shape[0]
    one_hot = (flat_ids[:, None] == jnp.arange(experts, dtype=jnp.int32)[None, :]).astype(jnp.int32)
    slot_rank = jnp.sum((jnp.cumsum(one_hot, axis=0) - one_hot) * one_hot, axis=1)
    slot_index = flat_ids * capacity + slot_rank
    source_of = (
        jnp.full((experts * capacity,), assign, jnp.int32)
        .at[slot_index]
        .set(jnp.arange(assign, dtype=jnp.int32))
    )
    token_of = source_of // top_count
    normed_pad = jnp.concatenate([normed, jnp.zeros((1, feat_width), jnp.bfloat16)], axis=0)
    grad_pad = jnp.concatenate(
        [grads.astype(jnp.float32), jnp.zeros((1, feat_width), jnp.float32)], axis=0
    )
    weight_pad = jnp.concatenate([weights.reshape(-1), jnp.zeros((1,), jnp.float32)])
    inputs_slab = normed_pad[token_of].reshape(experts, capacity, feat_width)
    grads_slab = (
        (weight_pad[source_of][:, None] * grad_pad[token_of])
        .astype(jnp.bfloat16)
        .reshape(experts, capacity, feat_width)
    )
    worked = expert_backward(
        slab_exchange(inputs_slab).reshape(experts * capacity, feat_width),
        slab_exchange(grads_slab).reshape(experts * capacity, feat_width),
        gate_up,
        down_proj,
    )
    returned = slab_exchange(worked.reshape(experts, capacity, feat_width))
    gathered = returned.reshape(experts * capacity, feat_width)[slot_index].astype(jnp.float32)
    return jnp.sum(gathered.reshape(tok_count, top_count, feat_width), axis=1)


def per_device(hidden_in, norm_gain, out_grad, expert_ids, route_weights, w_gate_up, w_down):
    tokens = hidden_in[0]
    gain_vector_row = norm_gain[0]
    incoming_gradient = out_grad[0]
    routes = expert_ids[0]
    weights = route_weights[0]
    gate_up = w_gate_up[0, 0]
    down_proj = w_down[0, 0]
    experts = lax.axis_size("expert")
    input_single_precision = tokens.astype(jnp.float32)
    inverse_root_mean = lax.rsqrt(
        jnp.mean(input_single_precision * input_single_precision, axis=-1, keepdims=True) + norm_eps
    )
    normalized_input = input_single_precision * inverse_root_mean
    rescaled_input = (normalized_input * gain_vector_row[None, :]).astype(jnp.bfloat16)
    block = tokens.size * 2
    held = gate_up.size * 2 + down_proj.size * 2 + (4 * experts + 9) * block
    if experts % 2 == 0 and held < vmem_bytes:
        chosen = routes[None, :, :] == jnp.arange(experts, dtype=jnp.int32)[:, None, None]
        weight_table = jnp.sum(jnp.where(chosen, weights[None, :, :], 0.0), axis=-1)
        dnorm = line_backward(
            rescaled_input, incoming_gradient, weight_table[:, None, :], gate_up, down_proj
        )
    else:
        dnorm = slab_backward(
            rescaled_input, incoming_gradient, routes, weights, gate_up, down_proj, experts
        )
    normalized_input_gradient = dnorm * gain_vector_row[None, :]
    projected_rows = jnp.mean(normalized_input_gradient * normalized_input, axis=-1, keepdims=True)
    section_gradient = (
        incoming_gradient.astype(jnp.float32)
        + inverse_root_mean * (normalized_input_gradient - normalized_input * projected_rows)
    ).astype(jnp.bfloat16)
    return shifted(section_gradient[None], "section", -1)


def solution(mesh):
    return jax.shard_map(
        per_device,
        mesh=mesh,
        in_specs=(
            P("section", "expert", None),
            P("section", None),
            P("section", "expert", None),
            P("section", "expert", None),
            P("section", "expert", None),
            P("section", "expert", None, None),
            P("section", "expert", None, None),
        ),
        out_specs=P("section", "expert", None),
        check_vma=False,
    )
```

```python
import functools
import jax
import jax.numpy as jnp
from jax import lax
from jax.experimental import pallas as pl
from jax.experimental.pallas import tpu as pltpu
from jax.sharding import PartitionSpec as P

glu_alpha = 1.702
norm_eps = 1e-05
vmem_bytes = 62 * 1024 * 1024
tile_width = 512


def spans(total, width):
    return [(start, min(start + width, total)) for start in range(0, total, width)]


def shifted(value, axis, steps):
    count = lax.axis_size(axis)
    pairs = [(source, (source + steps) % count) for source in range(count)]
    return lax.ppermute(value, axis, pairs)


def block_kernel(
    chips,
    hidden_hbm, gain_hbm, grad_hbm, wtab_hbm, gate_up_hbm, down_hbm, out_ref,
    xs, gs, gain, wtab, ws, gate_up, down, pre, act, res, cross_in, line_in,
    next_hidden, next_grad, next_gain, next_sum, inverse,
    load_sems, ahead_send, ahead_recv, sum_send, sum_recv, recv_x, recv_g, recv_w, send_w,
    up_x, up_g, dn_x, dn_g, cr_x, cr_g,
    cross_recv, cross_send, line_recv, line_send,
):
    me = lax.axis_index("expert")
    section = lax.axis_index("section")
    sections = lax.axis_size("section")
    preceding = (section + sections - 1) % sections
    following = (section + 1) % sections
    p = me // 2
    c = me % 2
    other = 1 - c
    count = 2 * chips
    rows, width = hidden_hbm.shape[1:]
    half = down_hbm.shape[0]
    out_spans = spans(width, tile_width)

    def device(chip, core):
        return {"expert": 2 * chip + core}

    load_x = pltpu.make_async_copy(hidden_hbm.at[0], xs.at[me], load_sems.at[0])
    load_g = pltpu.make_async_copy(grad_hbm.at[0], gs.at[me], load_sems.at[1])
    load_w = pltpu.make_async_copy(wtab_hbm, wtab, load_sems.at[2])
    load_gate_up = pltpu.make_async_copy(gate_up_hbm, gate_up, load_sems.at[3])
    load_down = pltpu.make_async_copy(down_hbm, down, load_sems.at[4])
    load_gain = pltpu.make_async_copy(gain_hbm, gain, load_sems.at[5])
    load_x.start()
    load_gain.start()
    load_g.start()
    load_w.start()
    load_gate_up.start()
    load_down.start()

    barrier = pltpu.get_barrier_semaphore()

    @pl.loop(1, count)
    def _(step):
        pl.semaphore_signal(barrier, inc=1, device_id={"expert": (me + step) % count})

    for neighbour in (preceding, following):
        pl.semaphore_signal(barrier, inc=1, device_id={"section": neighbour})

    load_x.wait()
    load_gain.wait()

    @pl.loop(0, rows // 16)
    def _(r):
        part = pl.ds(r * 16, 16)
        wide = xs[me, part, :].astype(jnp.float32)
        scale = lax.rsqrt(jnp.mean(wide * wide, axis=-1, keepdims=True) + norm_eps)
        xs[me, part, :] = (wide * scale * gain[...]).astype(jnp.bfloat16)

    pl.semaphore_wait(barrier, count + 1)

    def ahead_copy(number, source, target):
        return pltpu.make_async_remote_copy(
            src_ref=source, dst_ref=target,
            send_sem=ahead_send.at[number], recv_sem=ahead_recv.at[number],
            device_id={"section": preceding},
        )

    ahead = [
        ahead_copy(0, hidden_hbm.at[0], next_hidden),
        ahead_copy(1, grad_hbm.at[0], next_grad),
        ahead_copy(2, gain_hbm, next_gain),
    ]

    def sum_copy(t):
        first, last = out_spans[t]
        return pltpu.make_async_remote_copy(
            src_ref=res.at[me, :, pl.ds(first, last - first)],
            dst_ref=next_sum.at[:, pl.ds(first, last - first)],
            send_sem=sum_send.at[t], recv_sem=sum_recv.at[t],
            device_id={"section": preceding},
        )

    def gather_copy(buf, slot, send, recv, chip, core):
        return pltpu.make_async_remote_copy(
            src_ref=buf.at[slot], dst_ref=buf.at[slot],
            send_sem=send.at[slot], recv_sem=recv.at[slot],
            device_id=device(chip, core),
        )

    def weight_copy(target):
        return pltpu.make_async_remote_copy(
            src_ref=wtab.at[target], dst_ref=ws.at[me],
            send_sem=send_w.at[target], recv_sem=recv_w.at[me],
            device_id={"expert": target},
        )

    def weight_arrival(source):
        return pltpu.make_async_remote_copy(
            src_ref=wtab.at[source], dst_ref=ws.at[source],
            send_sem=send_w.at[source], recv_sem=recv_w.at[source],
            device_id={"expert": source},
        )

    def up_copy(buf, slot, send, recv):
        return gather_copy(buf, slot, send, recv, jnp.minimum(p + 1, chips - 1), c)

    def down_copy(buf, slot, send, recv):
        return gather_copy(buf, slot, send, recv, jnp.maximum(p - 1, 0), c)

    def core_copy(buf, slot, send, recv):
        return gather_copy(buf, slot, send, recv, p, other)

    def send_own(buf, up_sem, dn_sem, recv):
        @pl.when(p < chips - 1)
        def _():
            up_copy(buf, me, up_sem, recv).start()

        @pl.when(p > 0)
        def _():
            down_copy(buf, me, dn_sem, recv).start()

    def pass_on(k, buf, up_sem, dn_sem, cr_sem, recv):
        @pl.when(p - k >= 0)
        def _():
            slot = 2 * (p - k) + c
            core_copy(buf, slot, cr_sem, recv).wait_recv()
            core_copy(buf, slot, cr_sem, recv).start()

            @pl.when(p < chips - 1)
            def _():
                up_copy(buf, slot, up_sem, recv).start()

        @pl.when(p + k < chips)
        def _():
            slot = 2 * (p + k) + c
            core_copy(buf, slot, cr_sem, recv).wait_recv()
            core_copy(buf, slot, cr_sem, recv).start()

            @pl.when(p > 0)
            def _():
                down_copy(buf, slot, dn_sem, recv).start()

    def cross_copy(q, t):
        first, last = out_spans[t]
        return pltpu.make_async_remote_copy(
            src_ref=res.at[2 * q + other, :, pl.ds(first, last - first)],
            dst_ref=cross_in.at[q, :, pl.ds(first, last - first)],
            send_sem=cross_send.at[q, t], recv_sem=cross_recv.at[q, t],
            device_id=device(p, other),
        )

    def cross_arrival(q, t):
        return cross_copy(q, t)

    def line_copy(q, t):
        first, last = out_spans[t]
        toward = jnp.where(q > p, jnp.minimum(p + 1, chips - 1), jnp.maximum(p - 1, 0))
        slot = jnp.where(q > p, 0, 1)
        return pltpu.make_async_remote_copy(
            src_ref=res.at[2 * q + c, :, pl.ds(first, last - first)],
            dst_ref=line_in.at[slot, q, :, pl.ds(first, last - first)],
            send_sem=line_send.at[q, t], recv_sem=line_recv.at[slot, q, t],
            device_id=device(toward, c),
        )

    def line_arrival(slot, q, t):
        first, last = out_spans[t]
        return pltpu.make_async_remote_copy(
            src_ref=res.at[2 * q + c, :, pl.ds(first, last - first)],
            dst_ref=line_in.at[slot, q, :, pl.ds(first, last - first)],
            send_sem=line_send.at[q, t], recv_sem=line_recv.at[slot, q, t],
            device_id=device(p, other),
        )

    def combine(q, t):
        first, last = out_spans[t]
        cross_arrival(q, t).wait_recv()
        summed = res[2 * q + c, :, first:last].astype(jnp.float32) + cross_in[
            q, :, first:last
        ].astype(jnp.float32)
        res[2 * q + c, :, first:last] = summed.astype(jnp.bfloat16)
        starts = ((p == chips - 1) & (q < p)) | ((p == 0) & (q > p))

        @pl.when(starts)
        def _():
            line_copy(q, t).start()

    core_copy(xs, me, cr_x, recv_x).start()
    send_own(xs, up_x, dn_x, recv_x)
    load_g.wait()
    core_copy(gs, me, cr_g, recv_g).start()
    for copy in ahead:
        copy.start()
    load_w.wait()

    @pl.loop(1, count)
    def _(step):
        weight_copy((me + step) % count).start()

    ws[pl.ds(me, 1)] = wtab[pl.ds(me, 1)]
    load_gate_up.wait()
    load_down.wait()

    @pl.loop(1, count)
    def _(step):
        weight_arrival((me + step) % count).wait_recv()

    def forward_part(q):
        core_copy(xs, 2 * q + other, cr_x, recv_x).wait_recv()
        inputs = xs[pl.ds(2 * q, 2)].reshape(2 * rows, width)
        for first, last in spans(2 * half, 512):
            pre[:, first:last] = jnp.dot(
                inputs, gate_up[:, first:last], preferred_element_type=jnp.float32
            )

    def backward_part(q):
        core_copy(gs, 2 * q + other, cr_g, recv_g).wait_recv()
        diagonal = lax.broadcasted_iota(jnp.int32, (rows, rows), 0) == lax.broadcasted_iota(
            jnp.int32, (rows, rows), 1
        )
        for core in range(2):
            across = jnp.broadcast_to(ws[2 * q + core], (rows, rows))
            column = jnp.sum(jnp.where(diagonal, across, 0.0), axis=1, keepdims=True)
            act[core * rows:(core + 1) * rows, :] = (
                column * gs[2 * q + core].astype(jnp.float32)
            ).astype(jnp.bfloat16)
        for first, last in spans(half, 512):
            dact = lax.dot_general(
                act[...], down[first:last, :], (((1,), (1,)), ((), ())),
                preferred_element_type=jnp.float32,
            )
            gate = pre[:, first:last]
            up_part = pre[:, half + first:half + last]
            sig = jax.nn.sigmoid(glu_alpha * gate)
            pre[:, first:last] = dact * (up_part + 1.0) * (
                sig + glu_alpha * gate * sig * (1.0 - sig)
            )
            pre[:, half + first:half + last] = dact * gate * sig
        act[...] = pre[...].astype(jnp.bfloat16)
        for t, (first, last) in enumerate(out_spans):
            part = lax.dot_general(
                act[...], gate_up[first:last, :], (((1,), (1,)), ((), ())),
                preferred_element_type=jnp.float32,
            ).astype(jnp.bfloat16)
            res[pl.ds(2 * q, 2), :, first:last] = part.reshape(2, rows, last - first)
            cross_copy(q, t).start()
            if t > 0:
                combine(q, t - 1)
        combine(q, len(out_spans) - 1)

    low = p < chips // 2

    def chunk_of(k, first_turn):
        return jnp.where(low == first_turn, p + k, p - k)

    def inside(q):
        return (q >= 0) & (q < chips)

    @pl.loop(0, 2 * chips - 1)
    def _(i):
        k = (i + 1) // 2
        leading = i % 2 == 1
        q = chunk_of(k, leading)
        valid = inside(q)
        paired = inside(chunk_of(k - 1, False)) & (k >= 2)

        @pl.when(valid)
        def _():
            forward_part(q)

        @pl.when((leading & jnp.logical_not(paired)) | (jnp.logical_not(leading) & valid & (i > 0)))
        def _():
            pass_on(jnp.where(leading, k, k + 1), gs, up_g, dn_g, cr_g, recv_g)

        @pl.when(i == 0)
        def _():
            send_own(gs, up_g, dn_g, recv_g)

        @pl.when(valid)
        def _():
            backward_part(q)

        @pl.when(leading | (i == 0))
        def _():
            pass_on(k + 1, xs, up_x, dn_x, cr_x, recv_x)

    def relay(slot, q, t):
        first, last = out_spans[t]
        line_arrival(slot, q, t).wait_recv()
        summed = res[2 * q + c, :, first:last].astype(jnp.float32) + line_in[
            slot, q, :, first:last
        ].astype(jnp.float32)
        res[2 * q + c, :, first:last] = summed.astype(jnp.bfloat16)
        line_copy(q, t).start()

    inner = (p > 0) & (p < chips - 1)

    def relay_all(distance):
        for t in range(len(out_spans)):
            for turn in range(2):
                slot = jnp.where(low, turn, 1 - turn)
                q = jnp.where(slot == 0, distance, chips - 1 - distance)
                onward = jnp.where(slot == 0, q > p, q < p)

                @pl.when(inner & onward)
                def _(slot=slot, q=q, t=t):
                    relay(slot, q, t)

    for distance in range(1, chips - 1):
        relay_all(distance)

    for copy in ahead:
        copy.wait_recv()

    @pl.loop(0, rows // 16)
    def _(r):
        part = pl.ds(r * 16, 16)
        wide = next_hidden[part, :].astype(jnp.float32)
        inverse[part, :] = lax.rsqrt(jnp.mean(wide * wide, axis=-1, keepdims=True) + norm_eps)

    for t, (first, last) in enumerate(out_spans):
        for slot in range(2):
            @pl.when((p > 0) if slot == 0 else (p < chips - 1))
            def _(slot=slot, t=t, first=first, last=last):
                line_arrival(slot, p, t).wait_recv()

        below = jnp.where(p > 0, line_in[0, p, :, first:last].astype(jnp.float32), 0.0)
        above = jnp.where(p < chips - 1, line_in[1, p, :, first:last].astype(jnp.float32), 0.0)
        res[me, :, first:last] = (
            res[me, :, first:last].astype(jnp.float32) + below + above
        ).astype(jnp.bfloat16)
        sum_copy(t).start()

    relay_all(chips - 1)

    scale = inverse[...]
    projected = jnp.zeros((rows, 1), jnp.float32)
    for t, (first, last) in enumerate(out_spans):
        sum_copy(t).wait_recv()
        slope = next_sum[:, first:last].astype(jnp.float32) * next_gain[:, first:last]
        unit = next_hidden[:, first:last].astype(jnp.float32) * scale
        projected += jnp.sum(slope * unit, axis=1, keepdims=True)
    projected = projected / width
    for first, last in out_spans:
        slope = next_sum[:, first:last].astype(jnp.float32) * next_gain[:, first:last]
        unit = next_hidden[:, first:last].astype(jnp.float32) * scale
        out_ref[0, :, first:last] = (
            next_grad[:, first:last].astype(jnp.float32) + scale * (slope - unit * projected)
        ).astype(jnp.bfloat16)

    for copy in ahead:
        copy.wait_send()
    for t in range(len(out_spans)):
        sum_copy(t).wait_send()

    @pl.loop(1, count)
    def _(step):
        weight_copy((me + step) % count).wait_send()

    @pl.loop(0, chips)
    def _(q):
        slot = 2 * q + c
        core_copy(xs, slot, cr_x, recv_x).wait_send()
        core_copy(gs, slot, cr_g, recv_g).wait_send()

        @pl.when((q <= p) & (p < chips - 1))
        def _():
            up_copy(xs, slot, up_x, recv_x).wait_send()
            up_copy(gs, slot, up_g, recv_g).wait_send()

        @pl.when((q >= p) & (p > 0))
        def _():
            down_copy(xs, slot, dn_x, recv_x).wait_send()
            down_copy(gs, slot, dn_g, recv_g).wait_send()

        for t in range(len(out_spans)):
            cross_copy(q, t).wait_send()

            @pl.when(q != p)
            def _(t=t):
                line_copy(q, t).wait_send()


def line_backward(hidden, gains, grads, weight_table, gate_up, down_proj):
    count = weight_table.shape[0]
    chips = count // 2
    rows, width = hidden.shape[1:]
    half = down_proj.shape[0]
    pieces = len(spans(width, tile_width))
    dma = pltpu.SemaphoreType.DMA
    flops = 2 * count * rows * width * 5 * half
    return pl.pallas_call(
        functools.partial(block_kernel, chips),
        out_shape=jax.ShapeDtypeStruct((1, rows, width), jnp.bfloat16),
        in_specs=[pl.BlockSpec(memory_space=pl.ANY)] * 6,
        out_specs=pl.BlockSpec(memory_space=pltpu.VMEM),
        scratch_shapes=[
            pltpu.VMEM((count, rows, width), jnp.bfloat16),
            pltpu.VMEM((count, rows, width), jnp.bfloat16),
            pltpu.VMEM((1, width), jnp.float32),
            pltpu.VMEM((count, 1, rows), jnp.float32),
            pltpu.VMEM((count, 1, rows), jnp.float32),
            pltpu.VMEM((width, 2 * half), jnp.bfloat16),
            pltpu.VMEM((half, width), jnp.bfloat16),
            pltpu.VMEM((2 * rows, 2 * half), jnp.float32),
            pltpu.VMEM((2 * rows, width), jnp.bfloat16),
            pltpu.VMEM((count, rows, width), jnp.bfloat16),
            pltpu.VMEM((chips, rows, width), jnp.bfloat16),
            pltpu.VMEM((2, chips, rows, width), jnp.bfloat16),
            pltpu.VMEM((rows, width), jnp.bfloat16),
            pltpu.VMEM((rows, width), jnp.bfloat16),
            pltpu.VMEM((1, width), jnp.float32),
            pltpu.VMEM((rows, width), jnp.bfloat16),
            pltpu.VMEM((rows, 1), jnp.float32),
            dma((6,)), dma((3,)), dma((3,)), dma((pieces,)), dma((pieces,)),
            dma((count,)), dma((count,)), dma((count,)), dma((count,)),
            dma((count,)), dma((count,)), dma((count,)), dma((count,)),
            dma((count,)), dma((count,)),
            dma((chips, pieces)), dma((chips, pieces)),
            dma((2, chips, pieces)), dma((chips, pieces)),
        ],
        compiler_params=pltpu.CompilerParams(
            collective_id=0, has_side_effects=True, vmem_limit_bytes=vmem_bytes
        ),
        cost_estimate=pl.CostEstimate(
            flops=flops, bytes_accessed=10 * half * width, transcendentals=0
        ),
    )(hidden, gains, grads, weight_table, gate_up, down_proj)


def expert_backward(rows_in, grad_rows, gate_up, down_proj):
    preact = jnp.dot(rows_in, gate_up, preferred_element_type=jnp.float32)
    dact = lax.dot_general(
        grad_rows, down_proj, (((1,), (1,)), ((), ())), preferred_element_type=jnp.float32
    )
    half = down_proj.shape[0]
    gate = preact[:, :half]
    up_part = preact[:, half:]
    sig = jax.nn.sigmoid(glu_alpha * gate)
    dgate = dact * (up_part + 1.0) * (sig + glu_alpha * gate * sig * (1.0 - sig))
    dup = dact * gate * sig
    dpre = jnp.concatenate([dgate, dup], axis=1).astype(jnp.bfloat16)
    result = lax.dot_general(
        dpre, gate_up, (((1,), (1,)), ((), ())), preferred_element_type=jnp.float32
    )
    return result.astype(jnp.bfloat16)


def slab_exchange(slab):
    return lax.all_to_all(slab, "expert", split_axis=0, concat_axis=0, tiled=True)


def slab_backward(normed, grads, routes, weights, gate_up, down_proj, experts):
    tok_count, feat_width = normed.shape
    top_count = routes.shape[1]
    capacity = max(2, tok_count * top_count * 5 // (4 * experts))
    flat_ids = routes.reshape(-1)
    assign = flat_ids.shape[0]
    one_hot = (flat_ids[:, None] == jnp.arange(experts, dtype=jnp.int32)[None, :]).astype(jnp.int32)
    slot_rank = jnp.sum((jnp.cumsum(one_hot, axis=0) - one_hot) * one_hot, axis=1)
    slot_index = flat_ids * capacity + slot_rank
    source_of = (
        jnp.full((experts * capacity,), assign, jnp.int32)
        .at[slot_index]
        .set(jnp.arange(assign, dtype=jnp.int32))
    )
    token_of = source_of // top_count
    normed_pad = jnp.concatenate([normed, jnp.zeros((1, feat_width), jnp.bfloat16)], axis=0)
    grad_pad = jnp.concatenate(
        [grads.astype(jnp.float32), jnp.zeros((1, feat_width), jnp.float32)], axis=0
    )
    weight_pad = jnp.concatenate([weights.reshape(-1), jnp.zeros((1,), jnp.float32)])
    inputs_slab = normed_pad[token_of].reshape(experts, capacity, feat_width)
    grads_slab = (
        (weight_pad[source_of][:, None] * grad_pad[token_of])
        .astype(jnp.bfloat16)
        .reshape(experts, capacity, feat_width)
    )
    worked = expert_backward(
        slab_exchange(inputs_slab).reshape(experts * capacity, feat_width),
        slab_exchange(grads_slab).reshape(experts * capacity, feat_width),
        gate_up,
        down_proj,
    )
    returned = slab_exchange(worked.reshape(experts, capacity, feat_width))
    gathered = returned.reshape(experts * capacity, feat_width)[slot_index].astype(jnp.float32)
    return jnp.sum(gathered.reshape(tok_count, top_count, feat_width), axis=1)


def per_device(hidden_in, norm_gain, out_grad, expert_ids, route_weights, w_gate_up, w_down):
    tokens = hidden_in[0]
    gain_vector_row = norm_gain[0]
    incoming_gradient = out_grad[0]
    routes = expert_ids[0]
    weights = route_weights[0]
    gate_up = w_gate_up[0, 0]
    down_proj = w_down[0, 0]
    experts = lax.axis_size("expert")
    block = tokens.size * 2
    held = gate_up.size * 2 + down_proj.size * 2 + (4 * experts + 11) * block
    if experts % 2 == 0 and held < vmem_bytes:
        chosen = routes[None, :, :] == jnp.arange(experts, dtype=jnp.int32)[:, None, None]
        weight_table = jnp.sum(jnp.where(chosen, weights[None, :, :], 0.0), axis=-1)
        return line_backward(
            hidden_in, norm_gain, out_grad, weight_table[:, None, :], gate_up, down_proj
        )
    input_single_precision = tokens.astype(jnp.float32)
    inverse_root_mean = lax.rsqrt(
        jnp.mean(input_single_precision * input_single_precision, axis=-1, keepdims=True) + norm_eps
    )
    normalized_input = input_single_precision * inverse_root_mean
    rescaled_input = (normalized_input * gain_vector_row[None, :]).astype(jnp.bfloat16)
    dnorm = slab_backward(
        rescaled_input, incoming_gradient, routes, weights, gate_up, down_proj, experts
    )
    normalized_input_gradient = dnorm * gain_vector_row[None, :]
    projected_rows = jnp.mean(normalized_input_gradient * normalized_input, axis=-1, keepdims=True)
    section_gradient = (
        incoming_gradient.astype(jnp.float32)
        + inverse_root_mean * (normalized_input_gradient - normalized_input * projected_rows)
    ).astype(jnp.bfloat16)
    return shifted(section_gradient[None], "section", -1)


def solution(mesh):
    return jax.shard_map(
        per_device,
        mesh=mesh,
        in_specs=(
            P("section", "expert", None),
            P("section", None),
            P("section", "expert", None),
            P("section", "expert", None),
            P("section", "expert", None),
            P("section", "expert", None, None),
            P("section", "expert", None, None),
        ),
        out_specs=P("section", "expert", None),
        check_vma=False,
    )
```

```python
import functools
import jax
import jax.numpy as jnp
from jax import lax
from jax.experimental import pallas as pl
from jax.experimental.pallas import tpu as pltpu
from jax.sharding import PartitionSpec as P

glu_alpha = 1.702
norm_eps = 1e-05
vmem_bytes = 62 * 1024 * 1024
tile_width = 512


def spans(total, width):
    return [(start, min(start + width, total)) for start in range(0, total, width)]


def shifted(value, axis, steps):
    count = lax.axis_size(axis)
    pairs = [(source, (source + steps) % count) for source in range(count)]
    return lax.ppermute(value, axis, pairs)


def block_kernel(
    chips,
    hidden_hbm, gain_hbm, grad_hbm, wtab_hbm, gate_up_hbm, down_hbm, out_ref,
    xs, gs, gain, wtab, ws, gate_up, down, pre, act, res, cross_in, line_in,
    next_hidden, next_grad, next_gain, next_sum, inverse,
    load_sems, ahead_send, ahead_recv, sum_send, sum_recv, recv_x, recv_g, recv_w, send_w,
    up_x, up_g, dn_x, dn_g, cr_x, cr_g,
    cross_recv, cross_send, line_recv, line_send,
):
    me = lax.axis_index("expert")
    section = lax.axis_index("section")
    sections = lax.axis_size("section")
    preceding = (section + sections - 1) % sections
    following = (section + 1) % sections
    p = me // 2
    c = me % 2
    other = 1 - c
    count = 2 * chips
    width, rows = hidden_hbm.shape[1:]
    half = down_hbm.shape[0]
    out_spans = spans(width, tile_width)

    def device(chip, core):
        return {"expert": 2 * chip + core}

    load_x = pltpu.make_async_copy(hidden_hbm.at[0], act.at[:, pl.ds(0, rows)], load_sems.at[0])
    load_g = pltpu.make_async_copy(grad_hbm.at[0], gs.at[me], load_sems.at[1])
    load_w = pltpu.make_async_copy(wtab_hbm, wtab, load_sems.at[2])
    load_gate_up = pltpu.make_async_copy(gate_up_hbm, gate_up, load_sems.at[3])
    load_down = pltpu.make_async_copy(down_hbm, down, load_sems.at[4])
    load_gain = pltpu.make_async_copy(gain_hbm, gain, load_sems.at[5])
    load_x.start()
    load_gain.start()
    load_g.start()
    load_w.start()
    load_gate_up.start()
    load_down.start()

    barrier = pltpu.get_barrier_semaphore()

    @pl.loop(1, count)
    def _(step):
        pl.semaphore_signal(barrier, inc=1, device_id={"expert": (me + step) % count})

    for neighbour in (preceding, following):
        pl.semaphore_signal(barrier, inc=1, device_id={"section": neighbour})

    load_x.wait()
    load_gain.wait()

    squares = jnp.zeros((1, rows), jnp.float32)
    for first, last in spans(width, rows):
        wide = act[first:last, 0:rows].astype(jnp.float32)
        squares += jnp.sum(wide * wide, axis=0, keepdims=True)
    own_scale = lax.rsqrt(squares / width + norm_eps)
    for first, last in spans(width, rows):
        unit = act[first:last, 0:rows].astype(jnp.float32) * own_scale
        xs[me, :, first:last] = (unit.T * gain[:, first:last]).astype(jnp.bfloat16)

    pl.semaphore_wait(barrier, count + 1)

    def ahead_copy(number, source, target):
        return pltpu.make_async_remote_copy(
            src_ref=source, dst_ref=target,
            send_sem=ahead_send.at[number], recv_sem=ahead_recv.at[number],
            device_id={"section": preceding},
        )

    ahead = [
        ahead_copy(0, hidden_hbm.at[0], next_hidden),
        ahead_copy(1, grad_hbm.at[0], next_grad),
        ahead_copy(2, gain_hbm, next_gain),
    ]

    def sum_copy(t):
        first, last = out_spans[t]
        return pltpu.make_async_remote_copy(
            src_ref=res.at[me, pl.ds(first, last - first)],
            dst_ref=next_sum.at[pl.ds(first, last - first)],
            send_sem=sum_send.at[t], recv_sem=sum_recv.at[t],
            device_id={"section": preceding},
        )

    def gather_copy(buf, slot, send, recv, chip, core):
        return pltpu.make_async_remote_copy(
            src_ref=buf.at[slot], dst_ref=buf.at[slot],
            send_sem=send.at[slot], recv_sem=recv.at[slot],
            device_id=device(chip, core),
        )

    def weight_copy(target):
        return pltpu.make_async_remote_copy(
            src_ref=wtab.at[target], dst_ref=ws.at[me],
            send_sem=send_w.at[target], recv_sem=recv_w.at[me],
            device_id={"expert": target},
        )

    def weight_arrival(source):
        return pltpu.make_async_remote_copy(
            src_ref=wtab.at[source], dst_ref=ws.at[source],
            send_sem=send_w.at[source], recv_sem=recv_w.at[source],
            device_id={"expert": source},
        )

    def up_copy(buf, slot, send, recv):
        return gather_copy(buf, slot, send, recv, jnp.minimum(p + 1, chips - 1), c)

    def down_copy(buf, slot, send, recv):
        return gather_copy(buf, slot, send, recv, jnp.maximum(p - 1, 0), c)

    def core_copy(buf, slot, send, recv):
        return gather_copy(buf, slot, send, recv, p, other)

    def send_own(buf, up_sem, dn_sem, recv):
        @pl.when(p < chips - 1)
        def _():
            up_copy(buf, me, up_sem, recv).start()

        @pl.when(p > 0)
        def _():
            down_copy(buf, me, dn_sem, recv).start()

    def pass_on(k, buf, up_sem, dn_sem, cr_sem, recv):
        @pl.when(p - k >= 0)
        def _():
            slot = 2 * (p - k) + c
            core_copy(buf, slot, cr_sem, recv).wait_recv()
            core_copy(buf, slot, cr_sem, recv).start()

            @pl.when(p < chips - 1)
            def _():
                up_copy(buf, slot, up_sem, recv).start()

        @pl.when(p + k < chips)
        def _():
            slot = 2 * (p + k) + c
            core_copy(buf, slot, cr_sem, recv).wait_recv()
            core_copy(buf, slot, cr_sem, recv).start()

            @pl.when(p > 0)
            def _():
                down_copy(buf, slot, dn_sem, recv).start()

    def cross_copy(q, t):
        first, last = out_spans[t]
        return pltpu.make_async_remote_copy(
            src_ref=res.at[2 * q + other, pl.ds(first, last - first)],
            dst_ref=cross_in.at[q, pl.ds(first, last - first)],
            send_sem=cross_send.at[q, t], recv_sem=cross_recv.at[q, t],
            device_id=device(p, other),
        )

    def cross_arrival(q, t):
        return cross_copy(q, t)

    def line_copy(q, t):
        first, last = out_spans[t]
        toward = jnp.where(q > p, jnp.minimum(p + 1, chips - 1), jnp.maximum(p - 1, 0))
        slot = jnp.where(q > p, 0, 1)
        return pltpu.make_async_remote_copy(
            src_ref=res.at[2 * q + c, pl.ds(first, last - first)],
            dst_ref=line_in.at[slot, q, pl.ds(first, last - first)],
            send_sem=line_send.at[q, t], recv_sem=line_recv.at[slot, q, t],
            device_id=device(toward, c),
        )

    def line_arrival(slot, q, t):
        first, last = out_spans[t]
        return pltpu.make_async_remote_copy(
            src_ref=res.at[2 * q + c, pl.ds(first, last - first)],
            dst_ref=line_in.at[slot, q, pl.ds(first, last - first)],
            send_sem=line_send.at[q, t], recv_sem=line_recv.at[slot, q, t],
            device_id=device(p, other),
        )

    def combine(q, t):
        first, last = out_spans[t]
        cross_arrival(q, t).wait_recv()
        summed = res[2 * q + c, first:last, :].astype(jnp.float32) + cross_in[
            q, first:last, :
        ].astype(jnp.float32)
        res[2 * q + c, first:last, :] = summed.astype(jnp.bfloat16)
        starts = ((p == chips - 1) & (q < p)) | ((p == 0) & (q > p))

        @pl.when(starts)
        def _():
            line_copy(q, t).start()

    core_copy(xs, me, cr_x, recv_x).start()
    send_own(xs, up_x, dn_x, recv_x)
    load_g.wait()
    core_copy(gs, me, cr_g, recv_g).start()
    for copy in ahead:
        copy.start()
    load_w.wait()

    @pl.loop(1, count)
    def _(step):
        weight_copy((me + step) % count).start()

    ws[pl.ds(me, 1)] = wtab[pl.ds(me, 1)]
    load_gate_up.wait()
    load_down.wait()

    @pl.loop(1, count)
    def _(step):
        weight_arrival((me + step) % count).wait_recv()

    def forward_part(q):
        core_copy(xs, 2 * q + other, cr_x, recv_x).wait_recv()
        inputs = xs[pl.ds(2 * q, 2)].reshape(2 * rows, width)
        for first, last in spans(2 * half, 512):
            pre[first:last, :] = jnp.dot(
                inputs, gate_up[:, first:last], preferred_element_type=jnp.float32
            ).T

    def backward_part(q):
        core_copy(gs, 2 * q + other, cr_g, recv_g).wait_recv()
        for core in range(2):
            act[:, core * rows:(core + 1) * rows] = (
                ws[2 * q + core] * gs[2 * q + core].astype(jnp.float32)
            ).astype(jnp.bfloat16)
        for first, last in spans(half, 512):
            dact = jnp.dot(down[first:last, :], act[...], preferred_element_type=jnp.float32)
            gate = pre[first:last, :]
            up_part = pre[half + first:half + last, :]
            sig = jax.nn.sigmoid(glu_alpha * gate)
            pre[first:last, :] = dact * (up_part + 1.0) * (
                sig + glu_alpha * gate * sig * (1.0 - sig)
            )
            pre[half + first:half + last, :] = dact * gate * sig
        act[...] = pre[...].astype(jnp.bfloat16)
        for t, (first, last) in enumerate(out_spans):
            part = jnp.dot(
                gate_up[first:last, :], act[...], preferred_element_type=jnp.float32
            ).astype(jnp.bfloat16)
            for core in range(2):
                res[2 * q + core, first:last, :] = part[:, core * rows:(core + 1) * rows]
            cross_copy(q, t).start()
            if t > 0:
                combine(q, t - 1)
        combine(q, len(out_spans) - 1)

    low = p < chips // 2

    def chunk_of(k, first_turn):
        return jnp.where(low == first_turn, p + k, p - k)

    def inside(q):
        return (q >= 0) & (q < chips)

    @pl.loop(0, 2 * chips - 1)
    def _(i):
        k = (i + 1) // 2
        leading = i % 2 == 1
        q = chunk_of(k, leading)
        valid = inside(q)
        paired = inside(chunk_of(k - 1, False)) & (k >= 2)

        @pl.when(valid)
        def _():
            forward_part(q)

        @pl.when((leading & jnp.logical_not(paired)) | (jnp.logical_not(leading) & valid & (i > 0)))
        def _():
            pass_on(jnp.where(leading, k, k + 1), gs, up_g, dn_g, cr_g, recv_g)

        @pl.when(i == 0)
        def _():
            send_own(gs, up_g, dn_g, recv_g)

        @pl.when(valid)
        def _():
            backward_part(q)

        @pl.when(leading | (i == 0))
        def _():
            pass_on(k + 1, xs, up_x, dn_x, cr_x, recv_x)

    def relay(slot, q, t):
        first, last = out_spans[t]
        line_arrival(slot, q, t).wait_recv()
        summed = res[2 * q + c, first:last, :].astype(jnp.float32) + line_in[
            slot, q, first:last, :
        ].astype(jnp.float32)
        res[2 * q + c, first:last, :] = summed.astype(jnp.bfloat16)
        line_copy(q, t).start()

    inner = (p > 0) & (p < chips - 1)

    def relay_all(distance):
        for t in range(len(out_spans)):
            for turn in range(2):
                slot = jnp.where(low, turn, 1 - turn)
                q = jnp.where(slot == 0, distance, chips - 1 - distance)
                onward = jnp.where(slot == 0, q > p, q < p)

                @pl.when(inner & onward)
                def _(slot=slot, q=q, t=t):
                    relay(slot, q, t)

    for distance in range(1, chips - 1):
        relay_all(distance)

    for copy in ahead:
        copy.wait_recv()

    squares = jnp.zeros((1, rows), jnp.float32)
    for first, last in spans(width, rows):
        wide = next_hidden[first:last, :].astype(jnp.float32)
        squares += jnp.sum(wide * wide, axis=0, keepdims=True)
        across = jnp.broadcast_to(next_gain[:, first:last], (rows, last - first))
        pre[first:last, 0:rows] = across.T
    inverse[...] = lax.rsqrt(squares / width + norm_eps)

    for t, (first, last) in enumerate(out_spans):
        for slot in range(2):
            @pl.when((p > 0) if slot == 0 else (p < chips - 1))
            def _(slot=slot, t=t, first=first, last=last):
                line_arrival(slot, p, t).wait_recv()

        below = jnp.where(p > 0, line_in[0, p, first:last, :].astype(jnp.float32), 0.0)
        above = jnp.where(p < chips - 1, line_in[1, p, first:last, :].astype(jnp.float32), 0.0)
        res[me, first:last, :] = (
            res[me, first:last, :].astype(jnp.float32) + below + above
        ).astype(jnp.bfloat16)
        sum_copy(t).start()

    relay_all(chips - 1)

    scale = inverse[...]
    projected = jnp.zeros((1, rows), jnp.float32)
    for t, (first, last) in enumerate(out_spans):
        sum_copy(t).wait_recv()
        slope = next_sum[first:last, :].astype(jnp.float32) * pre[first:last, 0:rows]
        unit = next_hidden[first:last, :].astype(jnp.float32) * scale
        pre[first:last, rows:2 * rows] = slope
        projected += jnp.sum(slope * unit, axis=0, keepdims=True)
    projected = projected / width
    for first, last in out_spans:
        unit = next_hidden[first:last, :].astype(jnp.float32) * scale
        out_ref[0, first:last, :] = (
            next_grad[first:last, :].astype(jnp.float32)
            + scale * (pre[first:last, rows:2 * rows] - unit * projected)
        ).astype(jnp.bfloat16)

    for copy in ahead:
        copy.wait_send()
    for t in range(len(out_spans)):
        sum_copy(t).wait_send()

    @pl.loop(1, count)
    def _(step):
        weight_copy((me + step) % count).wait_send()

    @pl.loop(0, chips)
    def _(q):
        slot = 2 * q + c
        core_copy(xs, slot, cr_x, recv_x).wait_send()
        core_copy(gs, slot, cr_g, recv_g).wait_send()

        @pl.when((q <= p) & (p < chips - 1))
        def _():
            up_copy(xs, slot, up_x, recv_x).wait_send()
            up_copy(gs, slot, up_g, recv_g).wait_send()

        @pl.when((q >= p) & (p > 0))
        def _():
            down_copy(xs, slot, dn_x, recv_x).wait_send()
            down_copy(gs, slot, dn_g, recv_g).wait_send()

        for t in range(len(out_spans)):
            cross_copy(q, t).wait_send()

            @pl.when(q != p)
            def _(t=t):
                line_copy(q, t).wait_send()


def line_backward(hidden, gains, grads, weight_table, gate_up, down_proj):
    count = weight_table.shape[0]
    chips = count // 2
    width, rows = hidden.shape[1:]
    half = down_proj.shape[0]
    pieces = len(spans(width, tile_width))
    dma = pltpu.SemaphoreType.DMA
    flops = 2 * count * rows * width * 5 * half
    return pl.pallas_call(
        functools.partial(block_kernel, chips),
        out_shape=jax.ShapeDtypeStruct((1, width, rows), jnp.bfloat16),
        in_specs=[pl.BlockSpec(memory_space=pl.ANY)] * 6,
        out_specs=pl.BlockSpec(memory_space=pltpu.VMEM),
        scratch_shapes=[
            pltpu.VMEM((count, rows, width), jnp.bfloat16),
            pltpu.VMEM((count, width, rows), jnp.bfloat16),
            pltpu.VMEM((1, width), jnp.float32),
            pltpu.VMEM((count, 1, rows), jnp.float32),
            pltpu.VMEM((count, 1, rows), jnp.float32),
            pltpu.VMEM((width, 2 * half), jnp.bfloat16),
            pltpu.VMEM((half, width), jnp.bfloat16),
            pltpu.VMEM((max(width, 2 * half), 2 * rows), jnp.float32),
            pltpu.VMEM((width, 2 * rows), jnp.bfloat16),
            pltpu.VMEM((count, width, rows), jnp.bfloat16),
            pltpu.VMEM((chips, width, rows), jnp.bfloat16),
            pltpu.VMEM((2, chips, width, rows), jnp.bfloat16),
            pltpu.VMEM((width, rows), jnp.bfloat16),
            pltpu.VMEM((width, rows), jnp.bfloat16),
            pltpu.VMEM((1, width), jnp.float32),
            pltpu.VMEM((width, rows), jnp.bfloat16),
            pltpu.VMEM((1, rows), jnp.float32),
            dma((6,)), dma((3,)), dma((3,)), dma((pieces,)), dma((pieces,)),
            dma((count,)), dma((count,)), dma((count,)), dma((count,)),
            dma((count,)), dma((count,)), dma((count,)), dma((count,)),
            dma((count,)), dma((count,)),
            dma((chips, pieces)), dma((chips, pieces)),
            dma((2, chips, pieces)), dma((chips, pieces)),
        ],
        compiler_params=pltpu.CompilerParams(
            collective_id=0, has_side_effects=True, vmem_limit_bytes=vmem_bytes
        ),
        cost_estimate=pl.CostEstimate(
            flops=flops, bytes_accessed=10 * half * width, transcendentals=0
        ),
    )(hidden, gains, grads, weight_table, gate_up, down_proj)


def expert_backward(rows_in, grad_rows, gate_up, down_proj):
    preact = jnp.dot(rows_in, gate_up, preferred_element_type=jnp.float32)
    dact = lax.dot_general(
        grad_rows, down_proj, (((1,), (1,)), ((), ())), preferred_element_type=jnp.float32
    )
    half = down_proj.shape[0]
    gate = preact[:, :half]
    up_part = preact[:, half:]
    sig = jax.nn.sigmoid(glu_alpha * gate)
    dgate = dact * (up_part + 1.0) * (sig + glu_alpha * gate * sig * (1.0 - sig))
    dup = dact * gate * sig
    dpre = jnp.concatenate([dgate, dup], axis=1).astype(jnp.bfloat16)
    result = lax.dot_general(
        dpre, gate_up, (((1,), (1,)), ((), ())), preferred_element_type=jnp.float32
    )
    return result.astype(jnp.bfloat16)


def slab_exchange(slab):
    return lax.all_to_all(slab, "expert", split_axis=0, concat_axis=0, tiled=True)


def slab_backward(normed, grads, routes, weights, gate_up, down_proj, experts):
    tok_count, feat_width = normed.shape
    top_count = routes.shape[1]
    capacity = max(2, tok_count * top_count * 5 // (4 * experts))
    flat_ids = routes.reshape(-1)
    assign = flat_ids.shape[0]
    one_hot = (flat_ids[:, None] == jnp.arange(experts, dtype=jnp.int32)[None, :]).astype(jnp.int32)
    slot_rank = jnp.sum((jnp.cumsum(one_hot, axis=0) - one_hot) * one_hot, axis=1)
    slot_index = flat_ids * capacity + slot_rank
    source_of = (
        jnp.full((experts * capacity,), assign, jnp.int32)
        .at[slot_index]
        .set(jnp.arange(assign, dtype=jnp.int32))
    )
    token_of = source_of // top_count
    normed_pad = jnp.concatenate([normed, jnp.zeros((1, feat_width), jnp.bfloat16)], axis=0)
    grad_pad = jnp.concatenate(
        [grads.astype(jnp.float32), jnp.zeros((1, feat_width), jnp.float32)], axis=0
    )
    weight_pad = jnp.concatenate([weights.reshape(-1), jnp.zeros((1,), jnp.float32)])
    inputs_slab = normed_pad[token_of].reshape(experts, capacity, feat_width)
    grads_slab = (
        (weight_pad[source_of][:, None] * grad_pad[token_of])
        .astype(jnp.bfloat16)
        .reshape(experts, capacity, feat_width)
    )
    worked = expert_backward(
        slab_exchange(inputs_slab).reshape(experts * capacity, feat_width),
        slab_exchange(grads_slab).reshape(experts * capacity, feat_width),
        gate_up,
        down_proj,
    )
    returned = slab_exchange(worked.reshape(experts, capacity, feat_width))
    gathered = returned.reshape(experts * capacity, feat_width)[slot_index].astype(jnp.float32)
    return jnp.sum(gathered.reshape(tok_count, top_count, feat_width), axis=1)


def per_device(hidden_in, norm_gain, out_grad, expert_ids, route_weights, w_gate_up, w_down):
    tokens = hidden_in[0]
    gain_vector_row = norm_gain[0]
    incoming_gradient = out_grad[0]
    routes = expert_ids[0]
    weights = route_weights[0]
    gate_up = w_gate_up[0, 0]
    down_proj = w_down[0, 0]
    experts = lax.axis_size("expert")
    block = tokens.size * 2
    held = gate_up.size * 2 + down_proj.size * 2 + (4 * experts + 11) * block
    if experts % 2 == 0 and held < vmem_bytes:
        chosen = routes[None, :, :] == jnp.arange(experts, dtype=jnp.int32)[:, None, None]
        weight_table = jnp.sum(jnp.where(chosen, weights[None, :, :], 0.0), axis=-1)
        result = line_backward(
            hidden_in.transpose(0, 2, 1), norm_gain, out_grad.transpose(0, 2, 1),
            weight_table[:, None, :], gate_up, down_proj,
        )
        return result.transpose(0, 2, 1)
    input_single_precision = tokens.astype(jnp.float32)
    inverse_root_mean = lax.rsqrt(
        jnp.mean(input_single_precision * input_single_precision, axis=-1, keepdims=True) + norm_eps
    )
    normalized_input = input_single_precision * inverse_root_mean
    rescaled_input = (normalized_input * gain_vector_row[None, :]).astype(jnp.bfloat16)
    dnorm = slab_backward(
        rescaled_input, incoming_gradient, routes, weights, gate_up, down_proj, experts
    )
    normalized_input_gradient = dnorm * gain_vector_row[None, :]
    projected_rows = jnp.mean(normalized_input_gradient * normalized_input, axis=-1, keepdims=True)
    section_gradient = (
        incoming_gradient.astype(jnp.float32)
        + inverse_root_mean * (normalized_input_gradient - normalized_input * projected_rows)
    ).astype(jnp.bfloat16)
    return shifted(section_gradient[None], "section", -1)


def solution(mesh):
    return jax.shard_map(
        per_device,
        mesh=mesh,
        in_specs=(
            P("section", "expert", None),
            P("section", None),
            P("section", "expert", None),
            P("section", "expert", None),
            P("section", "expert", None),
            P("section", "expert", None, None),
            P("section", "expert", None, None),
        ),
        out_specs=P("section", "expert", None),
        check_vma=False,
    )
```

```python
import functools
import jax
import jax.numpy as jnp
from jax import lax
from jax.experimental import pallas as pl
from jax.experimental.pallas import tpu as pltpu
from jax.sharding import PartitionSpec as P

glu_alpha = 1.702
norm_eps = 1e-05
vmem_bytes = 62 * 1024 * 1024
tile_width = 512


def spans(total, width):
    return [(start, min(start + width, total)) for start in range(0, total, width)]


def shifted(value, axis, steps):
    count = lax.axis_size(axis)
    pairs = [(source, (source + steps) % count) for source in range(count)]
    return lax.ppermute(value, axis, pairs)


def block_kernel(
    chips,
    hidden_hbm, gain_hbm, grad_hbm, wtab_hbm, gate_up_hbm, down_hbm, out_ref,
    xs, gs, gain, wtab, ws, gate_up, down, pre, act, res, cross_in, line_in,
    next_hidden, next_grad, next_gain, next_sum, inverse,
    load_sems, ahead_send, ahead_recv, sum_send, sum_recv, recv_x, recv_g, recv_w, send_w,
    up_x, up_g, dn_x, dn_g, cr_x, cr_g,
    cross_recv, cross_send, line_recv, line_send,
):
    me = lax.axis_index("expert")
    section = lax.axis_index("section")
    sections = lax.axis_size("section")
    preceding = (section + sections - 1) % sections
    following = (section + 1) % sections
    p = me // 2
    c = me % 2
    other = 1 - c
    count = 2 * chips
    width, rows = hidden_hbm.shape[1:]
    half = down_hbm.shape[0]
    out_spans = spans(width, tile_width)

    def device(chip, core):
        return {"expert": 2 * chip + core}

    load_x = pltpu.make_async_copy(hidden_hbm.at[0], act.at[:, pl.ds(0, rows)], load_sems.at[0])
    load_g = pltpu.make_async_copy(grad_hbm.at[0], gs.at[me], load_sems.at[1])
    load_w = pltpu.make_async_copy(wtab_hbm, wtab, load_sems.at[2])
    load_gate_up = pltpu.make_async_copy(gate_up_hbm, gate_up, load_sems.at[3])
    load_down = pltpu.make_async_copy(down_hbm, down, load_sems.at[4])
    load_gain = pltpu.make_async_copy(gain_hbm, gain, load_sems.at[5])
    load_x.start()
    load_gain.start()
    load_g.start()
    load_w.start()
    load_gate_up.start()
    load_down.start()

    barrier = pltpu.get_barrier_semaphore()

    @pl.loop(1, count)
    def _(step):
        pl.semaphore_signal(barrier, inc=1, device_id={"expert": (me + step) % count})

    for neighbour in (preceding, following):
        pl.semaphore_signal(barrier, inc=1, device_id={"section": neighbour})

    load_x.wait()
    load_gain.wait()

    squares = jnp.zeros((1, rows), jnp.float32)
    for first, last in spans(width, rows):
        wide = act[first:last, 0:rows].astype(jnp.float32)
        squares += jnp.sum(wide * wide, axis=0, keepdims=True)
    own_scale = lax.rsqrt(squares / width + norm_eps)
    for first, last in spans(width, rows):
        unit = act[first:last, 0:rows].astype(jnp.float32) * own_scale
        xs[me, :, first:last] = (unit.T * gain[:, first:last]).astype(jnp.bfloat16)

    pl.semaphore_wait(barrier, count + 1)

    def ahead_copy(number, source, target):
        return pltpu.make_async_remote_copy(
            src_ref=source, dst_ref=target,
            send_sem=ahead_send.at[number], recv_sem=ahead_recv.at[number],
            device_id={"section": preceding},
        )

    ahead = [
        ahead_copy(0, hidden_hbm.at[0], next_hidden),
        ahead_copy(1, grad_hbm.at[0], next_grad),
        ahead_copy(2, gain_hbm, next_gain),
    ]

    def sum_copy(t):
        first, last = out_spans[t]
        return pltpu.make_async_remote_copy(
            src_ref=res.at[me, pl.ds(first, last - first)],
            dst_ref=next_sum.at[pl.ds(first, last - first)],
            send_sem=sum_send.at[t], recv_sem=sum_recv.at[t],
            device_id={"section": preceding},
        )

    def gather_copy(buf, slot, send, recv, chip, core):
        return pltpu.make_async_remote_copy(
            src_ref=buf.at[slot], dst_ref=buf.at[slot],
            send_sem=send.at[slot], recv_sem=recv.at[slot],
            device_id=device(chip, core),
        )

    def weight_copy(target):
        return pltpu.make_async_remote_copy(
            src_ref=wtab.at[target], dst_ref=ws.at[me],
            send_sem=send_w.at[target], recv_sem=recv_w.at[me],
            device_id={"expert": target},
        )

    def weight_arrival(source):
        return pltpu.make_async_remote_copy(
            src_ref=wtab.at[source], dst_ref=ws.at[source],
            send_sem=send_w.at[source], recv_sem=recv_w.at[source],
            device_id={"expert": source},
        )

    def up_copy(buf, slot, send, recv):
        return gather_copy(buf, slot, send, recv, jnp.minimum(p + 1, chips - 1), c)

    def down_copy(buf, slot, send, recv):
        return gather_copy(buf, slot, send, recv, jnp.maximum(p - 1, 0), c)

    def core_copy(buf, slot, send, recv):
        return gather_copy(buf, slot, send, recv, p, other)

    last_chip = chips - 1
    inner = (p > 0) & (p < last_chip)

    def send_own(buf, up_sem, dn_sem, recv, up_now, down_now):
        @pl.when((p < last_chip) & up_now)
        def _():
            up_copy(buf, me, up_sem, recv).start()

        @pl.when((p > 0) & down_now)
        def _():
            down_copy(buf, me, dn_sem, recv).start()

    def pass_on(k, buf, up_sem, dn_sem, cr_sem, recv):
        @pl.when(p - k >= 0)
        def _():
            slot = 2 * (p - k) + c
            core_copy(buf, slot, cr_sem, recv).wait_recv()
            core_copy(buf, slot, cr_sem, recv).start()

            @pl.when(p < chips - 1)
            def _():
                up_copy(buf, slot, up_sem, recv).start()

        @pl.when(p + k < chips)
        def _():
            slot = 2 * (p + k) + c
            core_copy(buf, slot, cr_sem, recv).wait_recv()
            core_copy(buf, slot, cr_sem, recv).start()

            @pl.when(p > 0)
            def _():
                down_copy(buf, slot, dn_sem, recv).start()

    def cross_copy(q, t):
        first, last = out_spans[t]
        return pltpu.make_async_remote_copy(
            src_ref=res.at[2 * q + other, pl.ds(first, last - first)],
            dst_ref=cross_in.at[q, pl.ds(first, last - first)],
            send_sem=cross_send.at[q, t], recv_sem=cross_recv.at[q, t],
            device_id=device(p, other),
        )

    def cross_arrival(q, t):
        return cross_copy(q, t)

    def line_copy(q, t):
        first, last = out_spans[t]
        toward = jnp.where(q > p, jnp.minimum(p + 1, chips - 1), jnp.maximum(p - 1, 0))
        slot = jnp.where(q > p, 0, 1)
        return pltpu.make_async_remote_copy(
            src_ref=res.at[2 * q + c, pl.ds(first, last - first)],
            dst_ref=line_in.at[slot, q, pl.ds(first, last - first)],
            send_sem=line_send.at[q, t], recv_sem=line_recv.at[slot, q, t],
            device_id=device(toward, c),
        )

    def line_arrival(slot, q, t):
        first, last = out_spans[t]
        return pltpu.make_async_remote_copy(
            src_ref=res.at[2 * q + c, pl.ds(first, last - first)],
            dst_ref=line_in.at[slot, q, pl.ds(first, last - first)],
            send_sem=line_send.at[q, t], recv_sem=line_recv.at[slot, q, t],
            device_id=device(p, other),
        )

    def combine(q, t):
        first, last = out_spans[t]
        cross_arrival(q, t).wait_recv()
        summed = res[2 * q + c, first:last, :].astype(jnp.float32) + cross_in[
            q, first:last, :
        ].astype(jnp.float32)
        res[2 * q + c, first:last, :] = summed.astype(jnp.bfloat16)
        starts = ((p == chips - 1) & (q < p)) | ((p == 0) & (q > p))

        @pl.when(starts)
        def _():
            line_copy(q, t).start()

    core_copy(xs, me, cr_x, recv_x).start()
    send_own(xs, up_x, dn_x, recv_x, p >= 0, p >= 0)
    load_g.wait()
    core_copy(gs, me, cr_g, recv_g).start()
    for copy in ahead:
        copy.start()
    load_w.wait()

    @pl.loop(1, count)
    def _(step):
        weight_copy((me + step) % count).start()

    ws[pl.ds(me, 1)] = wtab[pl.ds(me, 1)]
    load_gate_up.wait()
    load_down.wait()

    @pl.loop(1, count)
    def _(step):
        weight_arrival((me + step) % count).wait_recv()

    def forward_part(q):
        core_copy(xs, 2 * q + other, cr_x, recv_x).wait_recv()
        inputs = xs[pl.ds(2 * q, 2)].reshape(2 * rows, width)
        for first, last in spans(2 * half, 512):
            pre[first:last, :] = jnp.dot(
                inputs, gate_up[:, first:last], preferred_element_type=jnp.float32
            ).T

    def backward_part(q):
        core_copy(gs, 2 * q + other, cr_g, recv_g).wait_recv()
        for core in range(2):
            act[:, core * rows:(core + 1) * rows] = (
                ws[2 * q + core] * gs[2 * q + core].astype(jnp.float32)
            ).astype(jnp.bfloat16)
        for first, last in spans(half, 512):
            dact = jnp.dot(down[first:last, :], act[...], preferred_element_type=jnp.float32)
            gate = pre[first:last, :]
            up_part = pre[half + first:half + last, :]
            sig = jax.nn.sigmoid(glu_alpha * gate)
            pre[first:last, :] = dact * (up_part + 1.0) * (
                sig + glu_alpha * gate * sig * (1.0 - sig)
            )
            pre[half + first:half + last, :] = dact * gate * sig
        act[...] = pre[...].astype(jnp.bfloat16)
        for t, (first, last) in enumerate(out_spans):
            part = jnp.dot(
                gate_up[first:last, :], act[...], preferred_element_type=jnp.float32
            ).astype(jnp.bfloat16)
            for core in range(2):
                res[2 * q + core, first:last, :] = part[:, core * rows:(core + 1) * rows]
            cross_copy(q, t).start()
            if t > 0:
                combine(q, t - 1)
        combine(q, len(out_spans) - 1)

    low = p < chips // 2
    up_late = p == last_chip - 1
    down_late = p == 1

    def pass_x(k):
        pass_on(k, xs, up_x, dn_x, cr_x, recv_x)

    def pass_g(k):
        pass_on(k, gs, up_g, dn_g, cr_g, recv_g)

    def turn_value(i, values):
        chosen = values[-1]
        for number in range(len(values) - 2, -1, -1):
            chosen = jnp.where(i == number, values[number], chosen)
        return chosen

    @pl.loop(0, chips)
    def _(i):
        offset = jnp.where(
            inner, turn_value(i, (0, 1, -1, 2)), turn_value(i, (0, 2, 3, 1))
        )
        q = jnp.where(low, p + offset, p - offset)

        @pl.when(jnp.logical_not(inner) & ((i == 1) | (i == 2)))
        def _():
            pass_x(i + 1)

        forward_part(q)

        @pl.when(i == 0)
        def _():
            send_own(
                gs, up_g, dn_g, recv_g, jnp.logical_not(up_late), jnp.logical_not(down_late)
            )

        @pl.when((i == 0) | (inner & (i == 1)))
        def _():
            pass_x(i + 1)

        @pl.when(jnp.logical_not(inner) & (i > 0))
        def _():
            pass_g(turn_value(i, (0, 2, 3, 1)))

        backward_part(q)

        @pl.when(inner & (i < 2))
        def _():
            pass_g(i + 1)

        @pl.when(i == 1)
        def _():
            send_own(gs, up_g, dn_g, recv_g, up_late, down_late)

    def relay(slot, q, t):
        first, last = out_spans[t]
        line_arrival(slot, q, t).wait_recv()
        summed = res[2 * q + c, first:last, :].astype(jnp.float32) + line_in[
            slot, q, first:last, :
        ].astype(jnp.float32)
        res[2 * q + c, first:last, :] = summed.astype(jnp.bfloat16)
        line_copy(q, t).start()

    def relay_all(distance):
        for t in range(len(out_spans)):
            for turn in range(2):
                slot = jnp.where(low, turn, 1 - turn)
                q = jnp.where(slot == 0, distance, chips - 1 - distance)
                onward = jnp.where(slot == 0, q > p, q < p)

                @pl.when(inner & onward)
                def _(slot=slot, q=q, t=t):
                    relay(slot, q, t)

    for distance in range(1, chips):
        relay_all(distance)

    for copy in ahead:
        copy.wait_recv()

    squares = jnp.zeros((1, rows), jnp.float32)
    for first, last in spans(width, rows):
        wide = next_hidden[first:last, :].astype(jnp.float32)
        squares += jnp.sum(wide * wide, axis=0, keepdims=True)
        across = jnp.broadcast_to(next_gain[:, first:last], (rows, last - first))
        pre[first:last, 0:rows] = across.T
    inverse[...] = lax.rsqrt(squares / width + norm_eps)

    for t, (first, last) in enumerate(out_spans):
        for slot in range(2):
            @pl.when((p > 0) if slot == 0 else (p < chips - 1))
            def _(slot=slot, t=t, first=first, last=last):
                line_arrival(slot, p, t).wait_recv()

        below = jnp.where(p > 0, line_in[0, p, first:last, :].astype(jnp.float32), 0.0)
        above = jnp.where(p < chips - 1, line_in[1, p, first:last, :].astype(jnp.float32), 0.0)
        res[me, first:last, :] = (
            res[me, first:last, :].astype(jnp.float32) + below + above
        ).astype(jnp.bfloat16)
        sum_copy(t).start()

    scale = inverse[...]
    projected = jnp.zeros((1, rows), jnp.float32)
    for t, (first, last) in enumerate(out_spans):
        sum_copy(t).wait_recv()
        slope = next_sum[first:last, :].astype(jnp.float32) * pre[first:last, 0:rows]
        unit = next_hidden[first:last, :].astype(jnp.float32) * scale
        pre[first:last, rows:2 * rows] = slope
        projected += jnp.sum(slope * unit, axis=0, keepdims=True)
    projected = projected / width
    for first, last in out_spans:
        unit = next_hidden[first:last, :].astype(jnp.float32) * scale
        out_ref[0, first:last, :] = (
            next_grad[first:last, :].astype(jnp.float32)
            + scale * (pre[first:last, rows:2 * rows] - unit * projected)
        ).astype(jnp.bfloat16)

    for copy in ahead:
        copy.wait_send()
    for t in range(len(out_spans)):
        sum_copy(t).wait_send()

    @pl.loop(1, count)
    def _(step):
        weight_copy((me + step) % count).wait_send()

    @pl.loop(0, chips)
    def _(q):
        slot = 2 * q + c
        core_copy(xs, slot, cr_x, recv_x).wait_send()
        core_copy(gs, slot, cr_g, recv_g).wait_send()

        @pl.when((q <= p) & (p < chips - 1))
        def _():
            up_copy(xs, slot, up_x, recv_x).wait_send()
            up_copy(gs, slot, up_g, recv_g).wait_send()

        @pl.when((q >= p) & (p > 0))
        def _():
            down_copy(xs, slot, dn_x, recv_x).wait_send()
            down_copy(gs, slot, dn_g, recv_g).wait_send()

        for t in range(len(out_spans)):
            cross_copy(q, t).wait_send()

            @pl.when(q != p)
            def _(t=t):
                line_copy(q, t).wait_send()


def line_backward(hidden, gains, grads, weight_table, gate_up, down_proj):
    count = weight_table.shape[0]
    chips = count // 2
    width, rows = hidden.shape[1:]
    half = down_proj.shape[0]
    pieces = len(spans(width, tile_width))
    dma = pltpu.SemaphoreType.DMA
    flops = 2 * count * rows * width * 5 * half
    return pl.pallas_call(
        functools.partial(block_kernel, chips),
        out_shape=jax.ShapeDtypeStruct((1, width, rows), jnp.bfloat16),
        in_specs=[pl.BlockSpec(memory_space=pl.ANY)] * 6,
        out_specs=pl.BlockSpec(memory_space=pltpu.VMEM),
        scratch_shapes=[
            pltpu.VMEM((count, rows, width), jnp.bfloat16),
            pltpu.VMEM((count, width, rows), jnp.bfloat16),
            pltpu.VMEM((1, width), jnp.float32),
            pltpu.VMEM((count, 1, rows), jnp.float32),
            pltpu.VMEM((count, 1, rows), jnp.float32),
            pltpu.VMEM((width, 2 * half), jnp.bfloat16),
            pltpu.VMEM((half, width), jnp.bfloat16),
            pltpu.VMEM((max(width, 2 * half), 2 * rows), jnp.float32),
            pltpu.VMEM((width, 2 * rows), jnp.bfloat16),
            pltpu.VMEM((count, width, rows), jnp.bfloat16),
            pltpu.VMEM((chips, width, rows), jnp.bfloat16),
            pltpu.VMEM((2, chips, width, rows), jnp.bfloat16),
            pltpu.VMEM((width, rows), jnp.bfloat16),
            pltpu.VMEM((width, rows), jnp.bfloat16),
            pltpu.VMEM((1, width), jnp.float32),
            pltpu.VMEM((width, rows), jnp.bfloat16),
            pltpu.VMEM((1, rows), jnp.float32),
            dma((6,)), dma((3,)), dma((3,)), dma((pieces,)), dma((pieces,)),
            dma((count,)), dma((count,)), dma((count,)), dma((count,)),
            dma((count,)), dma((count,)), dma((count,)), dma((count,)),
            dma((count,)), dma((count,)),
            dma((chips, pieces)), dma((chips, pieces)),
            dma((2, chips, pieces)), dma((chips, pieces)),
        ],
        compiler_params=pltpu.CompilerParams(
            collective_id=0, has_side_effects=True, vmem_limit_bytes=vmem_bytes
        ),
        cost_estimate=pl.CostEstimate(
            flops=flops, bytes_accessed=10 * half * width, transcendentals=0
        ),
    )(hidden, gains, grads, weight_table, gate_up, down_proj)


def expert_backward(rows_in, grad_rows, gate_up, down_proj):
    preact = jnp.dot(rows_in, gate_up, preferred_element_type=jnp.float32)
    dact = lax.dot_general(
        grad_rows, down_proj, (((1,), (1,)), ((), ())), preferred_element_type=jnp.float32
    )
    half = down_proj.shape[0]
    gate = preact[:, :half]
    up_part = preact[:, half:]
    sig = jax.nn.sigmoid(glu_alpha * gate)
    dgate = dact * (up_part + 1.0) * (sig + glu_alpha * gate * sig * (1.0 - sig))
    dup = dact * gate * sig
    dpre = jnp.concatenate([dgate, dup], axis=1).astype(jnp.bfloat16)
    result = lax.dot_general(
        dpre, gate_up, (((1,), (1,)), ((), ())), preferred_element_type=jnp.float32
    )
    return result.astype(jnp.bfloat16)


def slab_exchange(slab):
    return lax.all_to_all(slab, "expert", split_axis=0, concat_axis=0, tiled=True)


def slab_backward(normed, grads, routes, weights, gate_up, down_proj, experts):
    tok_count, feat_width = normed.shape
    top_count = routes.shape[1]
    capacity = max(2, tok_count * top_count * 5 // (4 * experts))
    flat_ids = routes.reshape(-1)
    assign = flat_ids.shape[0]
    one_hot = (flat_ids[:, None] == jnp.arange(experts, dtype=jnp.int32)[None, :]).astype(jnp.int32)
    slot_rank = jnp.sum((jnp.cumsum(one_hot, axis=0) - one_hot) * one_hot, axis=1)
    slot_index = flat_ids * capacity + slot_rank
    source_of = (
        jnp.full((experts * capacity,), assign, jnp.int32)
        .at[slot_index]
        .set(jnp.arange(assign, dtype=jnp.int32))
    )
    token_of = source_of // top_count
    normed_pad = jnp.concatenate([normed, jnp.zeros((1, feat_width), jnp.bfloat16)], axis=0)
    grad_pad = jnp.concatenate(
        [grads.astype(jnp.float32), jnp.zeros((1, feat_width), jnp.float32)], axis=0
    )
    weight_pad = jnp.concatenate([weights.reshape(-1), jnp.zeros((1,), jnp.float32)])
    inputs_slab = normed_pad[token_of].reshape(experts, capacity, feat_width)
    grads_slab = (
        (weight_pad[source_of][:, None] * grad_pad[token_of])
        .astype(jnp.bfloat16)
        .reshape(experts, capacity, feat_width)
    )
    worked = expert_backward(
        slab_exchange(inputs_slab).reshape(experts * capacity, feat_width),
        slab_exchange(grads_slab).reshape(experts * capacity, feat_width),
        gate_up,
        down_proj,
    )
    returned = slab_exchange(worked.reshape(experts, capacity, feat_width))
    gathered = returned.reshape(experts * capacity, feat_width)[slot_index].astype(jnp.float32)
    return jnp.sum(gathered.reshape(tok_count, top_count, feat_width), axis=1)


def per_device(hidden_in, norm_gain, out_grad, expert_ids, route_weights, w_gate_up, w_down):
    tokens = hidden_in[0]
    gain_vector_row = norm_gain[0]
    incoming_gradient = out_grad[0]
    routes = expert_ids[0]
    weights = route_weights[0]
    gate_up = w_gate_up[0, 0]
    down_proj = w_down[0, 0]
    experts = lax.axis_size("expert")
    block = tokens.size * 2
    held = gate_up.size * 2 + down_proj.size * 2 + (4 * experts + 11) * block
    if experts == 8 and held < vmem_bytes:
        chosen = routes[None, :, :] == jnp.arange(experts, dtype=jnp.int32)[:, None, None]
        weight_table = jnp.sum(jnp.where(chosen, weights[None, :, :], 0.0), axis=-1)
        result = line_backward(
            hidden_in.transpose(0, 2, 1), norm_gain, out_grad.transpose(0, 2, 1),
            weight_table[:, None, :], gate_up, down_proj,
        )
        return result.transpose(0, 2, 1)
    input_single_precision = tokens.astype(jnp.float32)
    inverse_root_mean = lax.rsqrt(
        jnp.mean(input_single_precision * input_single_precision, axis=-1, keepdims=True) + norm_eps
    )
    normalized_input = input_single_precision * inverse_root_mean
    rescaled_input = (normalized_input * gain_vector_row[None, :]).astype(jnp.bfloat16)
    dnorm = slab_backward(
        rescaled_input, incoming_gradient, routes, weights, gate_up, down_proj, experts
    )
    normalized_input_gradient = dnorm * gain_vector_row[None, :]
    projected_rows = jnp.mean(normalized_input_gradient * normalized_input, axis=-1, keepdims=True)
    section_gradient = (
        incoming_gradient.astype(jnp.float32)
        + inverse_root_mean * (normalized_input_gradient - normalized_input * projected_rows)
    ).astype(jnp.bfloat16)
    return shifted(section_gradient[None], "section", -1)


def solution(mesh):
    return jax.shard_map(
        per_device,
        mesh=mesh,
        in_specs=(
            P("section", "expert", None),
            P("section", None),
            P("section", "expert", None),
            P("section", "expert", None),
            P("section", "expert", None),
            P("section", "expert", None, None),
            P("section", "expert", None, None),
        ),
        out_specs=P("section", "expert", None),
        check_vma=False,
    )
```

```python
import functools
import jax
import jax.numpy as jnp
from jax import lax
from jax.experimental import pallas as pl
from jax.experimental.pallas import tpu as pltpu
from jax.sharding import PartitionSpec as P

glu_alpha = 1.702
norm_eps = 1e-05
vmem_bytes = 62 * 1024 * 1024
tile_width = 512


def spans(total, width):
    return [(start, min(start + width, total)) for start in range(0, total, width)]


def shifted(value, axis, steps):
    count = lax.axis_size(axis)
    pairs = [(source, (source + steps) % count) for source in range(count)]
    return lax.ppermute(value, axis, pairs)


def block_kernel(
    chips,
    hidden_hbm, gain_hbm, grad_hbm, wtab_hbm, gate_up_hbm, down_hbm, out_ref,
    xs, gs, gain, wtab, ws, gate_up, down, pre, act, res, cross_in, line_in,
    next_hidden, next_grad, next_gain, next_sum, inverse,
    load_sems, ahead_send, ahead_recv, sum_send, sum_recv, recv_x, recv_g, recv_w, send_w,
    up_x, up_g, dn_x, dn_g, cr_x, cr_g,
    cross_recv, cross_send, line_recv, line_send,
):
    me = lax.axis_index("expert")
    section = lax.axis_index("section")
    sections = lax.axis_size("section")
    preceding = (section + sections - 1) % sections
    following = (section + 1) % sections
    p = me // 2
    c = me % 2
    other = 1 - c
    count = 2 * chips
    width, rows = hidden_hbm.shape[1:]
    half = down_hbm.shape[0]
    out_spans = spans(width, tile_width)

    def device(chip, core):
        return {"expert": 2 * chip + core}

    load_x = pltpu.make_async_copy(hidden_hbm.at[0], act.at[:, pl.ds(0, rows)], load_sems.at[0])
    load_g = pltpu.make_async_copy(grad_hbm.at[0], gs.at[me], load_sems.at[1])
    load_w = pltpu.make_async_copy(wtab_hbm, wtab, load_sems.at[2])
    load_gate_up = pltpu.make_async_copy(gate_up_hbm, gate_up, load_sems.at[3])
    load_down = pltpu.make_async_copy(down_hbm, down, load_sems.at[4])
    load_gain = pltpu.make_async_copy(gain_hbm, gain, load_sems.at[5])
    load_x.start()
    load_gain.start()
    load_g.start()
    load_w.start()
    load_gate_up.start()
    load_down.start()

    barrier = pltpu.get_barrier_semaphore()

    @pl.loop(1, count)
    def _(step):
        pl.semaphore_signal(barrier, inc=1, device_id={"expert": (me + step) % count})

    for neighbour in (preceding, following):
        pl.semaphore_signal(barrier, inc=1, device_id={"section": neighbour})

    load_x.wait()
    load_gain.wait()

    squares = jnp.zeros((1, rows), jnp.float32)
    for first, last in spans(width, rows):
        wide = act[first:last, 0:rows].astype(jnp.float32)
        squares += jnp.sum(wide * wide, axis=0, keepdims=True)
    own_scale = lax.rsqrt(squares / width + norm_eps)
    for first, last in spans(width, rows):
        unit = act[first:last, 0:rows].astype(jnp.float32) * own_scale
        xs[me, :, first:last] = (unit.T * gain[:, first:last]).astype(jnp.bfloat16)

    pl.semaphore_wait(barrier, count + 1)

    def ahead_copy(number, source, target):
        return pltpu.make_async_remote_copy(
            src_ref=source, dst_ref=target,
            send_sem=ahead_send.at[number], recv_sem=ahead_recv.at[number],
            device_id={"section": preceding},
        )

    ahead = [
        ahead_copy(0, hidden_hbm.at[0], next_hidden),
        ahead_copy(1, grad_hbm.at[0], next_grad),
        ahead_copy(2, gain_hbm, next_gain),
    ]

    def sum_copy(t):
        first, last = out_spans[t]
        return pltpu.make_async_remote_copy(
            src_ref=res.at[me, pl.ds(first, last - first)],
            dst_ref=next_sum.at[pl.ds(first, last - first)],
            send_sem=sum_send.at[t], recv_sem=sum_recv.at[t],
            device_id={"section": preceding},
        )

    def gather_copy(buf, slot, send, recv, chip, core):
        return pltpu.make_async_remote_copy(
            src_ref=buf.at[slot], dst_ref=buf.at[slot],
            send_sem=send.at[slot], recv_sem=recv.at[slot],
            device_id=device(chip, core),
        )

    def weight_copy(target):
        return pltpu.make_async_remote_copy(
            src_ref=wtab.at[target], dst_ref=ws.at[me],
            send_sem=send_w.at[target], recv_sem=recv_w.at[me],
            device_id={"expert": target},
        )

    def weight_arrival(source):
        return pltpu.make_async_remote_copy(
            src_ref=wtab.at[source], dst_ref=ws.at[source],
            send_sem=send_w.at[source], recv_sem=recv_w.at[source],
            device_id={"expert": source},
        )

    def up_copy(buf, slot, send, recv):
        return gather_copy(buf, slot, send, recv, jnp.minimum(p + 1, chips - 1), c)

    def down_copy(buf, slot, send, recv):
        return gather_copy(buf, slot, send, recv, jnp.maximum(p - 1, 0), c)

    def core_copy(buf, slot, send, recv):
        return gather_copy(buf, slot, send, recv, p, other)

    last_chip = chips - 1
    inner = (p > 0) & (p < last_chip)

    def send_own(buf, up_sem, dn_sem, recv):
        @pl.when(p < last_chip)
        def _():
            up_copy(buf, me, up_sem, recv).start()

        @pl.when(p > 0)
        def _():
            down_copy(buf, me, dn_sem, recv).start()

    def pass_on(k, buf, up_sem, dn_sem, cr_sem, recv):
        @pl.when(p - k >= 0)
        def _():
            slot = 2 * (p - k) + c
            core_copy(buf, slot, cr_sem, recv).wait_recv()
            core_copy(buf, slot, cr_sem, recv).start()

            @pl.when(p < chips - 1)
            def _():
                up_copy(buf, slot, up_sem, recv).start()

        @pl.when(p + k < chips)
        def _():
            slot = 2 * (p + k) + c
            core_copy(buf, slot, cr_sem, recv).wait_recv()
            core_copy(buf, slot, cr_sem, recv).start()

            @pl.when(p > 0)
            def _():
                down_copy(buf, slot, dn_sem, recv).start()

    def cross_copy(q, t):
        first, last = out_spans[t]
        return pltpu.make_async_remote_copy(
            src_ref=res.at[2 * q + other, pl.ds(first, last - first)],
            dst_ref=cross_in.at[q, pl.ds(first, last - first)],
            send_sem=cross_send.at[q, t], recv_sem=cross_recv.at[q, t],
            device_id=device(p, other),
        )

    def cross_arrival(q, t):
        return cross_copy(q, t)

    def line_copy(q, t):
        first, last = out_spans[t]
        toward = jnp.where(q > p, jnp.minimum(p + 1, chips - 1), jnp.maximum(p - 1, 0))
        slot = jnp.where(q > p, 0, 1)
        return pltpu.make_async_remote_copy(
            src_ref=res.at[2 * q + c, pl.ds(first, last - first)],
            dst_ref=line_in.at[slot, q, pl.ds(first, last - first)],
            send_sem=line_send.at[q, t], recv_sem=line_recv.at[slot, q, t],
            device_id=device(toward, c),
        )

    def line_arrival(slot, q, t):
        first, last = out_spans[t]
        return pltpu.make_async_remote_copy(
            src_ref=res.at[2 * q + c, pl.ds(first, last - first)],
            dst_ref=line_in.at[slot, q, pl.ds(first, last - first)],
            send_sem=line_send.at[q, t], recv_sem=line_recv.at[slot, q, t],
            device_id=device(p, other),
        )

    def combine(q, t):
        first, last = out_spans[t]
        cross_arrival(q, t).wait_recv()
        summed = res[2 * q + c, first:last, :].astype(jnp.float32) + cross_in[
            q, first:last, :
        ].astype(jnp.float32)
        res[2 * q + c, first:last, :] = summed.astype(jnp.bfloat16)
        starts = ((p == chips - 1) & (q < p)) | ((p == 0) & (q > p))

        @pl.when(starts)
        def _():
            line_copy(q, t).start()

    core_copy(xs, me, cr_x, recv_x).start()
    send_own(xs, up_x, dn_x, recv_x)
    load_g.wait()
    core_copy(gs, me, cr_g, recv_g).start()
    send_own(gs, up_g, dn_g, recv_g)
    for copy in ahead:
        copy.start()
    load_w.wait()

    @pl.loop(1, count)
    def _(step):
        weight_copy((me + step) % count).start()

    ws[pl.ds(me, 1)] = wtab[pl.ds(me, 1)]
    load_gate_up.wait()
    load_down.wait()

    @pl.loop(1, count)
    def _(step):
        weight_arrival((me + step) % count).wait_recv()

    def forward_part(q):
        core_copy(xs, 2 * q + other, cr_x, recv_x).wait_recv()
        inputs = xs[pl.ds(2 * q, 2)].reshape(2 * rows, width)
        for first, last in spans(2 * half, 512):
            pre[first:last, :] = jnp.dot(
                inputs, gate_up[:, first:last], preferred_element_type=jnp.float32
            ).T

    def backward_part(q):
        core_copy(gs, 2 * q + other, cr_g, recv_g).wait_recv()
        for core in range(2):
            act[:, core * rows:(core + 1) * rows] = (
                ws[2 * q + core] * gs[2 * q + core].astype(jnp.float32)
            ).astype(jnp.bfloat16)
        for first, last in spans(half, 512):
            dact = jnp.dot(down[first:last, :], act[...], preferred_element_type=jnp.float32)
            gate = pre[first:last, :]
            up_part = pre[half + first:half + last, :]
            sig = jax.nn.sigmoid(glu_alpha * gate)
            pre[first:last, :] = dact * (up_part + 1.0) * (
                sig + glu_alpha * gate * sig * (1.0 - sig)
            )
            pre[half + first:half + last, :] = dact * gate * sig
        act[...] = pre[...].astype(jnp.bfloat16)
        for t, (first, last) in enumerate(out_spans):
            part = jnp.dot(
                gate_up[first:last, :], act[...], preferred_element_type=jnp.float32
            ).astype(jnp.bfloat16)
            for core in range(2):
                res[2 * q + core, first:last, :] = part[:, core * rows:(core + 1) * rows]
            cross_copy(q, t).start()
            if t > 0:
                combine(q, t - 1)
        combine(q, len(out_spans) - 1)

    low = p < chips // 2

    def pass_x(k):
        pass_on(k, xs, up_x, dn_x, cr_x, recv_x)

    def pass_g(k):
        pass_on(k, gs, up_g, dn_g, cr_g, recv_g)

    def turn_value(i, values):
        chosen = values[-1]
        for number in range(len(values) - 2, -1, -1):
            chosen = jnp.where(i == number, values[number], chosen)
        return chosen

    @pl.loop(0, chips)
    def _(i):
        offset = jnp.where(
            inner, turn_value(i, (0, 1, -1, 2)), i
        )
        q = jnp.where(low, p + offset, p - offset)

        @pl.when(jnp.logical_not(inner) & (i > 1))
        def _():
            pass_x(i)

        forward_part(q)

        @pl.when((i == 0) | (inner & (i == 1)))
        def _():
            pass_x(i + 1)

        @pl.when(jnp.logical_not(inner) & (i > 0))
        def _():
            pass_g(i)

        backward_part(q)

        @pl.when(inner & (i < 2))
        def _():
            pass_g(i + 1)

    def relay(slot, q, t):
        first, last = out_spans[t]
        line_arrival(slot, q, t).wait_recv()
        summed = res[2 * q + c, first:last, :].astype(jnp.float32) + line_in[
            slot, q, first:last, :
        ].astype(jnp.float32)
        res[2 * q + c, first:last, :] = summed.astype(jnp.bfloat16)
        line_copy(q, t).start()

    def relay_all(distance):
        for t in range(len(out_spans)):
            for turn in range(2):
                slot = jnp.where(low, turn, 1 - turn)
                q = jnp.where(slot == 0, distance, chips - 1 - distance)
                onward = jnp.where(slot == 0, q > p, q < p)

                @pl.when(inner & onward)
                def _(slot=slot, q=q, t=t):
                    relay(slot, q, t)

    for distance in range(1, chips - 1):
        relay_all(distance)

    for copy in ahead:
        copy.wait_recv()

    squares = jnp.zeros((1, rows), jnp.float32)
    for first, last in spans(width, rows):
        wide = next_hidden[first:last, :].astype(jnp.float32)
        squares += jnp.sum(wide * wide, axis=0, keepdims=True)
        across = jnp.broadcast_to(next_gain[:, first:last], (rows, last - first))
        pre[first:last, 0:rows] = across.T
    inverse[...] = lax.rsqrt(squares / width + norm_eps)

    for t, (first, last) in enumerate(out_spans):
        for slot in range(2):
            @pl.when((p > 0) if slot == 0 else (p < chips - 1))
            def _(slot=slot, t=t, first=first, last=last):
                line_arrival(slot, p, t).wait_recv()

        below = jnp.where(p > 0, line_in[0, p, first:last, :].astype(jnp.float32), 0.0)
        above = jnp.where(p < chips - 1, line_in[1, p, first:last, :].astype(jnp.float32), 0.0)
        res[me, first:last, :] = (
            res[me, first:last, :].astype(jnp.float32) + below + above
        ).astype(jnp.bfloat16)
        sum_copy(t).start()

    relay_all(chips - 1)

    scale = inverse[...]
    projected = jnp.zeros((1, rows), jnp.float32)
    for t, (first, last) in enumerate(out_spans):
        sum_copy(t).wait_recv()
        slope = next_sum[first:last, :].astype(jnp.float32) * pre[first:last, 0:rows]
        unit = next_hidden[first:last, :].astype(jnp.float32) * scale
        pre[first:last, rows:2 * rows] = slope
        projected += jnp.sum(slope * unit, axis=0, keepdims=True)
    projected = projected / width
    for first, last in out_spans:
        unit = next_hidden[first:last, :].astype(jnp.float32) * scale
        out_ref[0, first:last, :] = (
            next_grad[first:last, :].astype(jnp.float32)
            + scale * (pre[first:last, rows:2 * rows] - unit * projected)
        ).astype(jnp.bfloat16)

    for copy in ahead:
        copy.wait_send()
    for t in range(len(out_spans)):
        sum_copy(t).wait_send()

    @pl.loop(1, count)
    def _(step):
        weight_copy((me + step) % count).wait_send()

    @pl.loop(0, chips)
    def _(q):
        slot = 2 * q + c
        core_copy(xs, slot, cr_x, recv_x).wait_send()
        core_copy(gs, slot, cr_g, recv_g).wait_send()

        @pl.when((q <= p) & (p < chips - 1))
        def _():
            up_copy(xs, slot, up_x, recv_x).wait_send()
            up_copy(gs, slot, up_g, recv_g).wait_send()

        @pl.when((q >= p) & (p > 0))
        def _():
            down_copy(xs, slot, dn_x, recv_x).wait_send()
            down_copy(gs, slot, dn_g, recv_g).wait_send()

        for t in range(len(out_spans)):
            cross_copy(q, t).wait_send()

            @pl.when(q != p)
            def _(t=t):
                line_copy(q, t).wait_send()


def line_backward(hidden, gains, grads, weight_table, gate_up, down_proj):
    count = weight_table.shape[0]
    chips = count // 2
    width, rows = hidden.shape[1:]
    half = down_proj.shape[0]
    pieces = len(spans(width, tile_width))
    dma = pltpu.SemaphoreType.DMA
    flops = 2 * count * rows * width * 5 * half
    return pl.pallas_call(
        functools.partial(block_kernel, chips),
        out_shape=jax.ShapeDtypeStruct((1, width, rows), jnp.bfloat16),
        in_specs=[pl.BlockSpec(memory_space=pl.ANY)] * 6,
        out_specs=pl.BlockSpec(memory_space=pltpu.VMEM),
        scratch_shapes=[
            pltpu.VMEM((count, rows, width), jnp.bfloat16),
            pltpu.VMEM((count, width, rows), jnp.bfloat16),
            pltpu.VMEM((1, width), jnp.float32),
            pltpu.VMEM((count, 1, rows), jnp.float32),
            pltpu.VMEM((count, 1, rows), jnp.float32),
            pltpu.VMEM((width, 2 * half), jnp.bfloat16),
            pltpu.VMEM((half, width), jnp.bfloat16),
            pltpu.VMEM((max(width, 2 * half), 2 * rows), jnp.float32),
            pltpu.VMEM((width, 2 * rows), jnp.bfloat16),
            pltpu.VMEM((count, width, rows), jnp.bfloat16),
            pltpu.VMEM((chips, width, rows), jnp.bfloat16),
            pltpu.VMEM((2, chips, width, rows), jnp.bfloat16),
            pltpu.VMEM((width, rows), jnp.bfloat16),
            pltpu.VMEM((width, rows), jnp.bfloat16),
            pltpu.VMEM((1, width), jnp.float32),
            pltpu.VMEM((width, rows), jnp.bfloat16),
            pltpu.VMEM((1, rows), jnp.float32),
            dma((6,)), dma((3,)), dma((3,)), dma((pieces,)), dma((pieces,)),
            dma((count,)), dma((count,)), dma((count,)), dma((count,)),
            dma((count,)), dma((count,)), dma((count,)), dma((count,)),
            dma((count,)), dma((count,)),
            dma((chips, pieces)), dma((chips, pieces)),
            dma((2, chips, pieces)), dma((chips, pieces)),
        ],
        compiler_params=pltpu.CompilerParams(
            collective_id=0, has_side_effects=True, vmem_limit_bytes=vmem_bytes
        ),
        cost_estimate=pl.CostEstimate(
            flops=flops, bytes_accessed=10 * half * width, transcendentals=0
        ),
    )(hidden, gains, grads, weight_table, gate_up, down_proj)


def expert_backward(rows_in, grad_rows, gate_up, down_proj):
    preact = jnp.dot(rows_in, gate_up, preferred_element_type=jnp.float32)
    dact = lax.dot_general(
        grad_rows, down_proj, (((1,), (1,)), ((), ())), preferred_element_type=jnp.float32
    )
    half = down_proj.shape[0]
    gate = preact[:, :half]
    up_part = preact[:, half:]
    sig = jax.nn.sigmoid(glu_alpha * gate)
    dgate = dact * (up_part + 1.0) * (sig + glu_alpha * gate * sig * (1.0 - sig))
    dup = dact * gate * sig
    dpre = jnp.concatenate([dgate, dup], axis=1).astype(jnp.bfloat16)
    result = lax.dot_general(
        dpre, gate_up, (((1,), (1,)), ((), ())), preferred_element_type=jnp.float32
    )
    return result.astype(jnp.bfloat16)


def slab_exchange(slab):
    return lax.all_to_all(slab, "expert", split_axis=0, concat_axis=0, tiled=True)


def slab_backward(normed, grads, routes, weights, gate_up, down_proj, experts):
    tok_count, feat_width = normed.shape
    top_count = routes.shape[1]
    capacity = max(2, tok_count * top_count * 5 // (4 * experts))
    flat_ids = routes.reshape(-1)
    assign = flat_ids.shape[0]
    one_hot = (flat_ids[:, None] == jnp.arange(experts, dtype=jnp.int32)[None, :]).astype(jnp.int32)
    slot_rank = jnp.sum((jnp.cumsum(one_hot, axis=0) - one_hot) * one_hot, axis=1)
    slot_index = flat_ids * capacity + slot_rank
    source_of = (
        jnp.full((experts * capacity,), assign, jnp.int32)
        .at[slot_index]
        .set(jnp.arange(assign, dtype=jnp.int32))
    )
    token_of = source_of // top_count
    normed_pad = jnp.concatenate([normed, jnp.zeros((1, feat_width), jnp.bfloat16)], axis=0)
    grad_pad = jnp.concatenate(
        [grads.astype(jnp.float32), jnp.zeros((1, feat_width), jnp.float32)], axis=0
    )
    weight_pad = jnp.concatenate([weights.reshape(-1), jnp.zeros((1,), jnp.float32)])
    inputs_slab = normed_pad[token_of].reshape(experts, capacity, feat_width)
    grads_slab = (
        (weight_pad[source_of][:, None] * grad_pad[token_of])
        .astype(jnp.bfloat16)
        .reshape(experts, capacity, feat_width)
    )
    worked = expert_backward(
        slab_exchange(inputs_slab).reshape(experts * capacity, feat_width),
        slab_exchange(grads_slab).reshape(experts * capacity, feat_width),
        gate_up,
        down_proj,
    )
    returned = slab_exchange(worked.reshape(experts, capacity, feat_width))
    gathered = returned.reshape(experts * capacity, feat_width)[slot_index].astype(jnp.float32)
    return jnp.sum(gathered.reshape(tok_count, top_count, feat_width), axis=1)


def per_device(hidden_in, norm_gain, out_grad, expert_ids, route_weights, w_gate_up, w_down):
    tokens = hidden_in[0]
    gain_vector_row = norm_gain[0]
    incoming_gradient = out_grad[0]
    routes = expert_ids[0]
    weights = route_weights[0]
    gate_up = w_gate_up[0, 0]
    down_proj = w_down[0, 0]
    experts = lax.axis_size("expert")
    block = tokens.size * 2
    held = gate_up.size * 2 + down_proj.size * 2 + (4 * experts + 11) * block
    if experts == 8 and held < vmem_bytes:
        chosen = routes[None, :, :] == jnp.arange(experts, dtype=jnp.int32)[:, None, None]
        weight_table = jnp.sum(jnp.where(chosen, weights[None, :, :], 0.0), axis=-1)
        result = line_backward(
            hidden_in.transpose(0, 2, 1), norm_gain, out_grad.transpose(0, 2, 1),
            weight_table[:, None, :], gate_up, down_proj,
        )
        return result.transpose(0, 2, 1)
    input_single_precision = tokens.astype(jnp.float32)
    inverse_root_mean = lax.rsqrt(
        jnp.mean(input_single_precision * input_single_precision, axis=-1, keepdims=True) + norm_eps
    )
    normalized_input = input_single_precision * inverse_root_mean
    rescaled_input = (normalized_input * gain_vector_row[None, :]).astype(jnp.bfloat16)
    dnorm = slab_backward(
        rescaled_input, incoming_gradient, routes, weights, gate_up, down_proj, experts
    )
    normalized_input_gradient = dnorm * gain_vector_row[None, :]
    projected_rows = jnp.mean(normalized_input_gradient * normalized_input, axis=-1, keepdims=True)
    section_gradient = (
        incoming_gradient.astype(jnp.float32)
        + inverse_root_mean * (normalized_input_gradient - normalized_input * projected_rows)
    ).astype(jnp.bfloat16)
    return shifted(section_gradient[None], "section", -1)


def solution(mesh):
    return jax.shard_map(
        per_device,
        mesh=mesh,
        in_specs=(
            P("section", "expert", None),
            P("section", None),
            P("section", "expert", None),
            P("section", "expert", None),
            P("section", "expert", None),
            P("section", "expert", None, None),
            P("section", "expert", None, None),
        ),
        out_specs=P("section", "expert", None),
        check_vma=False,
    )
```
